32 devices in a mesh: seq: 16 (over z, y, x), eig: 2 (over core).
Axes of the slice: x: 2, y: 2, z: 4, core: 2. Of those that a mesh axis runs over, the one named last changes fastest.
Arguments:
- train_in: bfloat16 [2048, 5120], P('seq'), may hold values from -6 to 6
- train_out: bfloat16 [2048, 13824], P('seq'), may hold values from -6 to 6
- query_in: bfloat16 [16, 5120], P('seq'), may hold values from -6 to 6
- query_out: bfloat16 [16, 13824], P('seq'), may hold values from -6 to 6
- input_basis: bfloat16 [5120, 5120], P('seq', 'eig'), may hold values from -0.078125 to 0.078125
- output_basis: bfloat16 [13824, 6912], P('seq', 'eig'), may hold values from -0.0546875 to 0.0546875
- corrected: bfloat16 [5120, 6912], P('seq', 'eig'), may hold values from 0.0099487305 to 10
- train_seq: int32 [2048], P('seq'), may hold values from 0 to 1
- query_order: int32 [16], P('seq'), may hold values from 0 to 15, each once
Outputs:
- scores: float32 [32, 16], P('seq')
The draws below stay inside these ranges and needn't reach their ends.
Inputs may be any that keep to these rules, and one draw needn't show every extreme that they name: query_order holds every number of 0 to 15 once, so each query has 1 token.
All inputs are finite; a program needn't handle non-finite values.
Results may differ from the reference program's by a relative error of at most 0.025.
Values may be sent and summed in bfloat16 or wider, within the bound.
No kernel may reach another device: no remote copies, remote signals or barrier semaphores. Data moves between devices by JAX's collectives and lax.ppermute only.
A program may use at most 192 MiB of HBM per device.

```python
import math
import jax
import jax.numpy as jnp
from jax import lax

DIN = 5120
DOUT = 13824
EIGOUT = 6912
TOK_DEV = 128
QTOK_DEV = 1
SEQ_DEV = 2
QUERIES = 16
TOKENS = 2048
QTOKENS = 16
N_SEQ = 16


def place_ends(entries, own_key, smallest, high):
    extent = entries.shape
    index_at = [jax.random.randint(jax.random.fold_in(own_key, axis), (), 0, extent[axis]) for axis in range(len(extent))]
    entries = entries.at[tuple(index_at)].set(smallest)
    longest = extent.index(max(extent))
    index_at[longest] = (index_at[longest] + 1) % extent[longest]
    return entries.at[tuple(index_at)].set(high)


def block_levels(own_key, shape, pieces, smallest, top_value):
    loudness, own = 1.0, jax.random.fold_in(own_key, 6)
    for axis_at, parts in pieces:
        draws = jnp.exp(jax.random.uniform(jax.random.fold_in(own, axis_at), (parts,), jnp.float32, smallest / len(pieces), top_value / len(pieces)))
        loudness = loudness * jnp.repeat(draws, shape[axis_at] // parts).reshape([-1 if axis == axis_at else 1 for axis in range(len(shape))])
    return loudness


def gaussian(stream_key, extent, spread, bound, split=(), held_as=jnp.bfloat16):
    entries = spread * jax.random.normal(stream_key, extent, jnp.float32)
    if split:
        entries = entries * block_levels(stream_key, extent, split, -0.22, 0.18)
    return jnp.clip(entries, -bound, bound).astype(held_as)


def setup_inputs(seed: int = 0) -> dict:
    splits = jax.random.split(jax.random.key(seed), 10)
    train_in = gaussian(splits[0], (TOKENS, DIN), 1.0, 6.0, ((0, 16),))
    train_out = gaussian(splits[1], (TOKENS, DOUT), 1.0, 6.0, ((0, 16),))
    query_in = gaussian(splits[2], (QTOKENS, DIN), 1.0, 6.0, ((0, 16),))
    query_out = gaussian(splits[3], (QTOKENS, DOUT), 1.0, 6.0, ((0, 16),))
    input_basis = gaussian(splits[4], (DIN, DIN), DIN ** -0.5, 0.078125, ((0, 16), (1, 2)))
    output_basis = gaussian(splits[5], (DOUT, EIGOUT), DOUT ** -0.5, 0.0546875, ((0, 16), (1, 2)))
    corrected = jnp.clip(jnp.exp(math.log(10.0) - 6.912895 * jax.random.uniform(splits[6], (DIN, EIGOUT), jnp.float32) ** block_levels(splits[6], (DIN, EIGOUT), ((0, 16), (1, 2)), -0.2, 0.2)), 0.0099487305, 10.0).astype(jnp.bfloat16)
    train_seq = place_ends(jax.random.randint(splits[7], (TOKENS,), 0, SEQ_DEV), jax.random.fold_in(splits[7], 1), 0, SEQ_DEV - 1).astype(jnp.int32)
    query_order = jax.random.permutation(splits[8], QTOKENS).astype(jnp.int32)
    return {"train_in": train_in, "train_out": train_out, "query_in": query_in, "query_out": query_out, "input_basis": input_basis, "output_basis": output_basis, "corrected": corrected, "train_seq": train_seq, "query_order": query_order}


DAMPING = 0.1

def rotate(row_data, eigvecs):
    stride = eigvecs.shape[0] // N_SEQ

    def advance(running, block_index):
        row_start = (block_index * stride).astype(jnp.int32)
        left_cols = lax.dynamic_slice_in_dim(row_data, row_start, stride, 1)
        right_rows = lax.dynamic_slice_in_dim(eigvecs, row_start, stride, 0)
        partial_value = jnp.dot(left_cols, right_rows, preferred_element_type=jnp.float32)
        partial_value = lax.optimization_barrier(partial_value.astype(jnp.bfloat16)).astype(jnp.float32)
        return (running + partial_value, None)
    start_sum = jnp.zeros((row_data.shape[0], eigvecs.shape[1]), jnp.float32)
    running, _ = lax.scan(advance, start_sum, jnp.arange(N_SEQ, dtype=jnp.int32))
    return running.astype(jnp.bfloat16)

def reference(train_in, train_out, query_in, query_out, input_basis, output_basis, corrected, train_seq, query_order):
    rotated_in = rotate(train_in, input_basis)
    rotated_out = rotate(train_out, output_basis)
    query_a = rotate(query_in, input_basis)
    query_b = rotate(query_out, output_basis)
    one_hot = ((query_order % QUERIES)[:, None] == jnp.arange(QUERIES, dtype=jnp.int32)[None, :]).astype(jnp.float32)
    damped = corrected.astype(jnp.float32) + DAMPING
    query_float = query_b.astype(jnp.float32)

    def score_one(flat_index):
        group_index = flat_index // SEQ_DEV
        member = flat_index % SEQ_DEV
        row_start = (group_index * TOK_DEV).astype(jnp.int32)
        a_rows = lax.dynamic_slice_in_dim(rotated_in, row_start, TOK_DEV, 0)
        b_rows = lax.dynamic_slice_in_dim(rotated_out, row_start, TOK_DEV, 0)
        seq_ids = lax.dynamic_slice_in_dim(train_seq, row_start, TOK_DEV, 0)
        masked = jnp.where((seq_ids == member)[:, None], b_rows, jnp.zeros_like(b_rows))
        raw_grad = lax.dot_general(a_rows, masked, (((0,), (0,)), ((), ())), preferred_element_type=jnp.float32)
        scaled = (raw_grad / damped).astype(jnp.bfloat16)
        projected = jnp.dot(query_a, scaled, preferred_element_type=jnp.float32)
        per_token = lax.optimization_barrier(jnp.sum(projected * query_float, axis=1))
        return lax.optimization_barrier(jnp.sum(per_token[:, None] * one_hot, axis=0))
    raw_scores = lax.map(score_one, jnp.arange(N_SEQ * SEQ_DEV, dtype=jnp.int32))
    factor = 1.0 / jnp.sqrt(jnp.float32(DIN) * jnp.float32(EIGOUT) * (jnp.float32(TOK_DEV) / SEQ_DEV) * (jnp.float32(QTOK_DEV * N_SEQ) / QUERIES))
    return raw_scores * factor
```

```python
import functools
import math

import jax
import jax.numpy as jnp
from jax import lax
from jax.experimental import pallas as pl
from jax.experimental.pallas import tpu as pltpu
from jax.sharding import PartitionSpec as P

DIN = 5120
EIGOUT = 6912
TOK_DEV = 128
SEQ_DEV = 2
QUERIES = 16
DAMPING = 0.1
INNER = 4
F32 = jnp.float32
BF16 = jnp.bfloat16
NT = (((1,), (1,)), ((), ()))
VMEM = pl.BlockSpec(memory_space=pltpu.VMEM)
SMEM = pl.BlockSpec(memory_space=pltpu.SMEM)


def bits(count):
    return range(count.bit_length() - 1)


def pick(x, index, axis=0):
    return lax.dynamic_index_in_dim(x, index, axis, keepdims=False)


def swap(x, axis, mask):
    size = lax.axis_size(axis)
    return lax.ppermute(x, axis, [(i, i ^ mask) for i in range(size)])


def unxor(x, index):
    size = x.shape[0]
    for b in bits(size):
        pairs = x.reshape((size >> (b + 1), 2, 1 << b) + x.shape[1:])
        turned = jnp.concatenate([pairs[:, 1:], pairs[:, :1]], axis=1)
        x = jnp.where((index >> b) & 1 == 1, turned, pairs).reshape(x.shape)
    return x


def add(*terms):
    total = terms[0].astype(F32)
    for term in terms[1:]:
        total = total + term.astype(F32)
    return total.astype(BF16)


def group_rows(parts, e, index):
    shares = []
    for h in range(len(parts)):
        share = parts[0][index]
        for m in range(1, len(parts)):
            share = jnp.where((e ^ m) == h, parts[m][index], share)
        shares.append(share)
    return jnp.concatenate(shares, axis=0) if len(shares) > 1 else shares[0]


def rotate_in_kernel(n, blocks, position, *refs):
    where, query, basis, parts, out = refs[0], refs[1], refs[2], refs[3:-1], refs[-1]
    me, e = where[0], where[1]
    width = basis.shape[0] // blocks

    def store(group, product, lane):
        for k in range(blocks):
            out[k, group] = product[
                k * width : (k + 1) * width, lane * TOK_DEV : (lane + 1) * TOK_DEV
            ].astype(BF16)

    store(n, lax.dot_general(basis[...], query[...], NT, preferred_element_type=F32), 0)

    @pl.loop(0, n // 4)
    def _(step):
        rows = [group_rows(parts, e, position((step * 4 + p) ^ me)) for p in range(4)]
        product = lax.dot_general(
            basis[...], jnp.concatenate(rows, axis=0), NT, preferred_element_type=F32
        )
        for p in range(4):
            store(step * 4 + p, product, p)


def rotate_in(where, query, basis, parts, n, blocks, position):
    width = basis.shape[0] // blocks
    return pl.pallas_call(
        functools.partial(rotate_in_kernel, n, blocks, position),
        out_shape=jax.ShapeDtypeStruct((blocks, n + 1, width, TOK_DEV), BF16),
        in_specs=[SMEM] + [VMEM] * (2 + len(parts)),
        out_specs=VMEM,
        compiler_params=pltpu.CompilerParams(vmem_limit_bytes=40 << 20),
        cost_estimate=pl.CostEstimate(
            flops=2 * (n + 1) * TOK_DEV * basis.size,
            bytes_accessed=2 * (basis.size + 2 * n * TOK_DEV * basis.shape[1]),
            transcendentals=0,
        ),
    )(where, query, basis, *parts)


def rotate_out_kernel(chunk, outer, where, basis, *refs):
    parts, (sx, kx, sy, ky) = refs[:-4], refs[-4:]
    me, e = where[0], where[1]
    half = outer // 2
    rows = [group_rows(parts, e, (chunk * outer + p) ^ me) for p in range(outer)]
    product = lax.dot_general(
        basis[0], jnp.concatenate(rows, axis=0), NT, preferred_element_type=F32
    )
    low = [product[:, p * TOK_DEV : (p + 1) * TOK_DEV].astype(BF16) for p in range(half)]
    high = [
        product[:, p * TOK_DEV : (p + 1) * TOK_DEV].astype(BF16) for p in range(half, outer)
    ]

    def put(ref, place, values):
        for p, value in enumerate(values):
            ref[place, p] = value

    for r, (a, i, b, j) in enumerate(
        [(kx, 0, ky, 0), (sx, 0, ky, 1), (kx, 1, sy, 0), (sx, 1, sy, 1)]
    ):

        @pl.when(pl.program_id(0) == r)
        def _(a=a, i=i, b=b, j=j):
            put(a, i, low)
            put(b, j, high)


def rotate_out(where, basis, parts, chunk, outer):
    _, cols, depth = basis.shape
    half = outer // 2
    whole = jax.ShapeDtypeStruct((2, half, cols, TOK_DEV), BF16)
    kept = pl.BlockSpec(whole.shape, lambda r, w: (0, 0, 0, 0))
    return pl.pallas_call(
        functools.partial(rotate_out_kernel, chunk, outer),
        out_shape=[whole] * 4,
        grid_spec=pltpu.PrefetchScalarGridSpec(
            num_scalar_prefetch=1,
            grid=(INNER,),
            in_specs=[pl.BlockSpec((1, cols, depth), lambda r, w: (r ^ (w[0] % INNER), 0, 0))]
            + [pl.BlockSpec(part.shape, lambda r, w: (0, 0, 0)) for part in parts],
            out_specs=[kept] * 4,
        ),
        compiler_params=pltpu.CompilerParams(vmem_limit_bytes=40 << 20),
        cost_estimate=pl.CostEstimate(
            flops=2 * outer * TOK_DEV * basis.size,
            bytes_accessed=2 * (basis.size + outer * TOK_DEV * (INNER * cols + depth)),
            transcendentals=0,
        ),
    )(where, basis, *parts)


def score_kernel(chunk, outer, masks, where, b_ref, a_ref, inverse, query_b, seq, out):
    z = where[0] // INNER
    count, rows = a_ref.shape[0] - 1, a_ref.shape[1]
    tile = 256 if rows % 256 == 0 else 128
    for p, mask in enumerate(masks):
        place = z ^ mask
        group = chunk * outer + place
        for member in range(SEQ_DEV):
            b = jnp.where(seq[group] == member, b_ref[p].astype(F32), 0.0).astype(BF16)
            total = jnp.zeros((b.shape[0], TOK_DEV), F32)
            for start in range(0, rows, tile):
                grad = lax.dot_general(
                    b, a_ref[group, start : start + tile], NT, preferred_element_type=F32
                )
                scaled = (grad * inverse[:, start : start + tile]).astype(BF16)
                total = total + jnp.dot(
                    scaled, a_ref[count, start : start + tile], preferred_element_type=F32
                )
            out[place, member : member + 1] = jnp.sum(
                total * query_b[...], axis=0, keepdims=True
            )


def score(where, b, a, inverse, query_b, seq, chunk, outer, masks):
    cols, rows = inverse.shape
    return pl.pallas_call(
        functools.partial(score_kernel, chunk, outer, masks),
        out_shape=jax.ShapeDtypeStruct((outer, SEQ_DEV, TOK_DEV), F32),
        in_specs=[SMEM] + [VMEM] * 5,
        out_specs=VMEM,
        compiler_params=pltpu.CompilerParams(vmem_limit_bytes=48 << 20),
        cost_estimate=pl.CostEstimate(
            flops=8 * outer * SEQ_DEV * TOK_DEV * cols * rows,
            bytes_accessed=2 * (b.size + a.size + 2 * inverse.size),
            transcendentals=0,
        ),
    )(where, b, a, inverse, query_b, seq)


def body(
    train_in,
    train_out,
    query_in,
    query_out,
    input_basis,
    output_basis,
    corrected,
    train_seq,
    query_order,
):
    n, size = lax.axis_size("seq"), lax.axis_size("eig")
    outer = n // INNER
    me, e = lax.axis_index("seq"), lax.axis_index("eig")
    xy, z = me % INNER, me // INNER
    where = jnp.stack([me, e]).astype(jnp.int32)
    share = TOK_DEV // size
    query_rows = query_in.shape[0]
    depth_out, cols = output_basis.shape
    cols_own = cols // INNER
    rows_own = corrected.shape[0]
    rows_in = rows_own * INNER
    per_core = input_basis.shape[1] // rows_in

    own = lax.dynamic_slice_in_dim(train_out, e * share, share, 0)
    own = own.reshape(share, n, depth_out).transpose(1, 0, 2)
    out_rel = jnp.stack(
        [pick(own, me)] + [swap(pick(own, me ^ m), "seq", m) for m in range(1, n)]
    )
    out_parts = [out_rel] + [swap(out_rel, "eig", m) for m in range(1, size)]

    small = jnp.concatenate(
        [
            query_in,
            query_out,
            train_seq.astype(BF16).reshape(query_rows, -1),
            (query_order % QUERIES).astype(BF16)[:, None],
        ],
        axis=1,
    )
    small = lax.all_gather(small, "seq", axis=0, tiled=True)
    din, dout = query_in.shape[1], query_out.shape[1]
    seq = small[:, din + dout : -1].reshape(n, 1, TOK_DEV).astype(F32)
    labels = small[:, -1].astype(F32)
    hot = (labels[:, None] == jnp.arange(QUERIES, dtype=F32)[None, :]).astype(F32)
    queries = small.shape[0]

    blocks = input_basis.reshape(rows_own, per_core, INNER, rows_own).transpose(2, 0, 1, 3)
    blocks = blocks.reshape(INNER, rows_own, per_core * rows_own)
    basis_in = jnp.stack(
        [pick(blocks, xy)] + [swap(pick(blocks, xy ^ r), "seq", r) for r in range(1, INNER)]
    )
    basis_in = unxor(basis_in, xy).reshape(rows_in, -1).T

    own = lax.dynamic_slice_in_dim(train_in, e * share, share, 0)
    own = own.reshape(share, outer, rows_in).transpose(1, 0, 2)
    in_rel = jnp.stack(
        [pick(own, z)]
        + [swap(pick(own, z ^ m), "seq", m * INNER) for m in range(1, outer)]
    )
    in_rel = jnp.concatenate([in_rel] + [swap(in_rel, "seq", r) for r in range(1, INNER)])
    in_parts = [in_rel] + [swap(in_rel, "eig", m) for m in range(1, size)]
    query_rows_in = lax.dynamic_slice_in_dim(small, z * rows_in, rows_in, 1)
    query_rows_in = jnp.pad(query_rows_in, ((0, TOK_DEV - queries), (0, 0)))
    rotated = rotate_in(
        where,
        query_rows_in,
        basis_in,
        in_parts,
        n,
        per_core,
        lambda rel: (rel % INNER) * outer + rel // INNER,
    )
    rotated = rotated.reshape(per_core, n + 1, size, rows_own // size, TOK_DEV)
    rotated = jnp.stack(
        [pick(rotated, e, 2)]
        + [swap(pick(rotated, e ^ m, 2), "eig", m) for m in range(1, size)]
    )
    rotated = unxor(rotated, e).reshape((outer,) + rotated.shape[2:])
    for b in bits(outer):
        bit = (z >> b) & 1
        pairs = rotated.reshape((-1, 2) + rotated.shape[1:])
        rotated = add(
            pick(pairs, bit, 1), swap(pick(pairs, 1 - bit, 1), "seq", INNER << b)
        )
    rotated = rotated[0]
    rotated = jnp.stack([rotated] + [swap(rotated, "seq", r) for r in range(1, INNER)])
    rotated = jnp.stack([rotated] + [swap(rotated, "eig", m) for m in range(1, size)])
    full_a = unxor(rotated, e).transpose(2, 1, 0, 3, 4).reshape(n + 1, rows_in, TOK_DEV)

    blocks = corrected.reshape(rows_own, INNER, cols_own).transpose(1, 0, 2)
    piece = jnp.concatenate(
        [pick(blocks, xy)] + [swap(pick(blocks, xy ^ r), "seq", r) for r in range(1, INNER)]
    )
    inverse = 1.0 / (piece.T.astype(F32) + DAMPING)

    query_b = lax.dynamic_slice_in_dim(small, din + me * depth_out, depth_out, 1)
    query_b = jnp.dot(query_b, output_basis, preferred_element_type=F32).astype(BF16)
    for b in bits(n):
        query_b = add(query_b, swap(query_b, "seq", 1 << b))
    query_b = lax.dynamic_slice_in_dim(query_b, xy * cols_own, cols_own, 1)
    query_b = jnp.pad(query_b.astype(F32), ((0, TOK_DEV - queries), (0, 0))).T

    basis_out = output_basis.reshape(depth_out, INNER, cols_own).transpose(1, 2, 0)
    found = []
    for chunk in range(INNER):
        sx, kx, sy, ky = rotate_out(where, basis_out, out_parts, chunk, outer)
        rx, ry = swap(sx, "seq", 1), swap(sy, "seq", 2)
        low = add(kx[0], rx[0], swap(add(kx[1], rx[1]), "seq", 2))
        high = add(ky[0], ry[0], swap(add(ky[1], ry[1]), "seq", 1))
        held = jnp.concatenate([low, high])
        for b in bits(outer):
            bit = (z >> b) & 1
            pairs = held.reshape((-1, 2) + held.shape[1:])
            held = add(
                pick(pairs, bit, 1), swap(pick(pairs, 1 - bit, 1), "seq", INNER << b)
            )
        masks = [0]
        for b in reversed(bits(outer)):
            held = jnp.concatenate([held, swap(held, "seq", INNER << b)])
            masks = masks + [m | (1 << b) for m in masks]
        found.append(
            score(where, held, full_a, inverse, query_b, seq, chunk, outer, masks)
        )
    per_token = jnp.concatenate(found)[:, :, :queries]
    scores = jnp.sum(per_token[:, :, :, None] * hot[None, None], axis=2)
    scores = lax.all_to_all(scores, "seq", split_axis=0, concat_axis=0, tiled=True)
    scores = jnp.sum(scores, axis=0)
    for b in bits(size):
        scores = scores + swap(scores, "eig", 1 << b)
    factor = 1.0 / math.sqrt(DIN * EIGOUT * (TOK_DEV / SEQ_DEV) * (queries / QUERIES))
    return scores * factor


def solution(mesh):
    placed = (
        P("seq", None),
        P("seq", None),
        P("seq", None),
        P("seq", None),
        P("seq", "eig"),
        P("seq", "eig"),
        P("seq", "eig"),
        P("seq"),
        P("seq"),
    )
    return jax.shard_map(
        body, mesh=mesh, in_specs=placed, out_specs=P("seq", None), check_vma=False
    )
```

```python
import functools
import math

import jax
import jax.numpy as jnp
from jax import lax
from jax.experimental import pallas as pl
from jax.experimental.pallas import tpu as pltpu
from jax.sharding import PartitionSpec as P

DIN = 5120
EIGOUT = 6912
TOK_DEV = 128
SEQ_DEV = 2
QUERIES = 16
DAMPING = 0.1
INNER = 4
F32 = jnp.float32
BF16 = jnp.bfloat16
NT = (((1,), (1,)), ((), ()))
VMEM = pl.BlockSpec(memory_space=pltpu.VMEM)
SMEM = pl.BlockSpec(memory_space=pltpu.SMEM)


def bits(count):
    return range(count.bit_length() - 1)


def pick(x, index, axis=0):
    return lax.dynamic_index_in_dim(x, index, axis, keepdims=False)


def swap(x, axis, mask):
    size = lax.axis_size(axis)
    return lax.ppermute(x, axis, [(i, i ^ mask) for i in range(size)])


def unxor(x, index):
    size = x.shape[0]
    for b in bits(size):
        pairs = x.reshape((size >> (b + 1), 2, 1 << b) + x.shape[1:])
        turned = jnp.concatenate([pairs[:, 1:], pairs[:, :1]], axis=1)
        x = jnp.where((index >> b) & 1 == 1, turned, pairs).reshape(x.shape)
    return x


def after(x, *done):
    return lax.optimization_barrier((x,) + done)[0]


def add(*terms):
    total = terms[0].astype(F32)
    for term in terms[1:]:
        total = total + term.astype(F32)
    return total.astype(BF16)


def group_rows(parts, e, index):
    shares = []
    for h in range(len(parts)):
        share = parts[0][index]
        for m in range(1, len(parts)):
            share = jnp.where((e ^ m) == h, parts[m][index], share)
        shares.append(share)
    return jnp.concatenate(shares, axis=0) if len(shares) > 1 else shares[0]


def split_kernel(pieces, where, *refs):
    sources, outs = refs[: -len(pieces)], refs[-len(pieces) :]
    xy = where[0] % INNER
    for v in range(INNER):

        @pl.when(xy == v)
        def _(v=v):
            for r, out in enumerate(outs):
                at = 0
                for start, stop in pieces[r ^ v]:
                    for s, source in enumerate(sources):
                        out[s, :, at : at + stop - start] = source[:, start:stop]
                    at += stop - start


def split(where, sources, pieces):
    rows = sources[0].shape[0]
    width = sum(stop - start for start, stop in pieces[0])
    shape = jax.ShapeDtypeStruct((len(sources), rows, width), sources[0].dtype)
    return pl.pallas_call(
        functools.partial(split_kernel, pieces),
        out_shape=[shape] * len(pieces),
        in_specs=[SMEM] + [VMEM] * len(sources),
        out_specs=[VMEM] * len(pieces),
        compiler_params=pltpu.CompilerParams(vmem_limit_bytes=40 << 20),
        cost_estimate=pl.CostEstimate(
            flops=0, bytes_accessed=4 * len(sources) * sources[0].size, transcendentals=0
        ),
    )(where, *sources)


def invert_kernel(*refs):
    sources, out = refs[:-1], refs[-1]
    rows = sources[0].shape[1]
    for r, source in enumerate(sources):
        damped = source[0].astype(F32) + DAMPING
        out[:, r * rows : (r + 1) * rows] = (1.0 / damped).T


def invert(sources):
    _, rows, cols = sources[0].shape
    return pl.pallas_call(
        invert_kernel,
        out_shape=jax.ShapeDtypeStruct((cols, len(sources) * rows), F32),
        in_specs=[VMEM] * len(sources),
        out_specs=VMEM,
        compiler_params=pltpu.CompilerParams(vmem_limit_bytes=40 << 20),
        cost_estimate=pl.CostEstimate(
            flops=8 * rows * cols, bytes_accessed=24 * rows * cols, transcendentals=0
        ),
    )(*sources)


def rotate_in_kernel(n, blocks, outer, *refs):
    where, query, basis, parts, out = refs[0], refs[1], refs[2], refs[3:-1], refs[-1]
    me, e = where[0], where[1]
    width = basis.shape[0] // blocks

    def store(group, product, lane):
        for k in range(blocks):
            out[k, group] = product[
                k * width : (k + 1) * width, lane * TOK_DEV : (lane + 1) * TOK_DEV
            ].astype(BF16)

    store(n, lax.dot_general(basis[...], query[...], NT, preferred_element_type=F32), 0)

    @pl.loop(0, n // 4)
    def _(step):
        rows = []
        for p in range(4):
            rel = (step * 4 + p) ^ me
            rows.append(group_rows(parts, e, (rel % INNER) * outer + rel // INNER))
        product = lax.dot_general(
            basis[...], jnp.concatenate(rows, axis=0), NT, preferred_element_type=F32
        )
        for p in range(4):
            store(step * 4 + p, product, p)


def rotate_in(where, query, basis, parts, n, blocks, outer):
    width = basis.shape[0] // blocks
    return pl.pallas_call(
        functools.partial(rotate_in_kernel, n, blocks, outer),
        out_shape=jax.ShapeDtypeStruct((blocks, n + 1, width, TOK_DEV), BF16),
        in_specs=[SMEM] + [VMEM] * (2 + len(parts)),
        out_specs=VMEM,
        compiler_params=pltpu.CompilerParams(vmem_limit_bytes=40 << 20),
        cost_estimate=pl.CostEstimate(
            flops=2 * (n + 1) * TOK_DEV * basis.size,
            bytes_accessed=2 * (basis.size + 2 * n * TOK_DEV * basis.shape[1]),
            transcendentals=0,
        ),
    )(where, query, basis, *parts)


def rotate_out_kernel(chunk, outer, where, basis, *refs):
    parts, (sx, kx, sy, ky), rows = refs[:-5], refs[-5:-1], refs[-1]
    me, e = where[0], where[1]
    half = outer // 2

    @pl.when(pl.program_id(0) == 0)
    def _():
        for p in range(outer):
            rel = (chunk * outer + p) ^ me
            rows[p * TOK_DEV : (p + 1) * TOK_DEV] = group_rows(
                parts, e, (rel % INNER) * outer + rel // INNER
            )

    product = lax.dot_general(basis[0], rows[...], NT, preferred_element_type=F32)
    low = [product[:, p * TOK_DEV : (p + 1) * TOK_DEV].astype(BF16) for p in range(half)]
    high = [
        product[:, p * TOK_DEV : (p + 1) * TOK_DEV].astype(BF16) for p in range(half, outer)
    ]

    def put(ref, place, values):
        for p, value in enumerate(values):
            ref[place, p] = value

    for r, (a, i, b, j) in enumerate(
        [(kx, 0, ky, 0), (sx, 0, ky, 1), (kx, 1, sy, 0), (sx, 1, sy, 1)]
    ):

        @pl.when(pl.program_id(0) == r)
        def _(a=a, i=i, b=b, j=j):
            put(a, i, low)
            put(b, j, high)


def rotate_out(where, basis, parts, chunk, outer):
    _, cols, depth = basis.shape
    half = outer // 2
    whole = jax.ShapeDtypeStruct((2, half, cols, TOK_DEV), BF16)
    kept = pl.BlockSpec(whole.shape, lambda r, w: (0, 0, 0, 0))
    return pl.pallas_call(
        functools.partial(rotate_out_kernel, chunk, outer),
        out_shape=[whole] * 4,
        grid_spec=pltpu.PrefetchScalarGridSpec(
            num_scalar_prefetch=1,
            grid=(INNER,),
            in_specs=[pl.BlockSpec((1, cols, depth), lambda r, w: (r ^ (w[0] % INNER), 0, 0))]
            + [pl.BlockSpec(part.shape, lambda r, w: (0, 0, 0)) for part in parts],
            out_specs=[kept] * 4,
            scratch_shapes=[pltpu.VMEM((outer * TOK_DEV, depth), BF16)],
        ),
        compiler_params=pltpu.CompilerParams(vmem_limit_bytes=40 << 20),
        cost_estimate=pl.CostEstimate(
            flops=2 * outer * TOK_DEV * basis.size,
            bytes_accessed=2 * (basis.size + outer * TOK_DEV * (INNER * cols + depth)),
            transcendentals=0,
        ),
    )(where, basis, *parts)


def score_kernel(chunk, outer, masks, shares, where, b_ref, inverse, query_b, seq, *refs):
    a_refs, out, a_all = refs[:shares], refs[shares], refs[shares + 1]
    z, e = where[0] // INNER, where[1]
    count, rows = a_refs[0].shape[1] - 1, a_all.shape[1]
    width = a_refs[0].shape[2]
    tile = 256 if rows % 256 == 0 else 128

    def gather(group, slot):
        for r in range(INNER):
            for h in range(shares):
                a = a_refs[0][r, group]
                for m in range(1, shares):
                    a = jnp.where((e ^ m) == h, a_refs[m][r, group], a)
                start = (r * shares + h) * width
                a_all[slot, start : start + width] = a

    gather(count, len(masks))
    for p, mask in enumerate(masks):
        place = z ^ mask
        group = chunk * outer + place
        gather(group, p)
        for member in range(SEQ_DEV):
            b = jnp.where(seq[group] == member, b_ref[p].astype(F32), 0.0).astype(BF16)
            total = jnp.zeros((b.shape[0], TOK_DEV), F32)
            for start in range(0, rows, tile):
                grad = lax.dot_general(
                    b, a_all[p, start : start + tile], NT, preferred_element_type=F32
                )
                scaled = (grad * inverse[:, start : start + tile]).astype(BF16)
                total = total + jnp.dot(
                    scaled,
                    a_all[len(masks), start : start + tile],
                    preferred_element_type=F32,
                )
            out[p, member : member + 1] = jnp.sum(total * query_b[...], axis=0, keepdims=True)


def score(where, b, a_parts, inverse, query_b, seq, chunk, outer, masks):
    cols, rows = inverse.shape
    count = len(masks)
    return pl.pallas_call(
        functools.partial(score_kernel, chunk, outer, masks, len(a_parts)),
        out_shape=jax.ShapeDtypeStruct((count, SEQ_DEV, TOK_DEV), F32),
        in_specs=[SMEM] + [VMEM] * (4 + len(a_parts)),
        out_specs=VMEM,
        scratch_shapes=[pltpu.VMEM((count + 1, rows, TOK_DEV), BF16)],
        compiler_params=pltpu.CompilerParams(vmem_limit_bytes=48 << 20),
        cost_estimate=pl.CostEstimate(
            flops=16 * count * SEQ_DEV * TOK_DEV * cols * rows,
            bytes_accessed=2 * (b.size + 2 * a_parts[0].size + 2 * inverse.size),
            transcendentals=0,
        ),
    )(where, b, inverse, query_b, seq, *a_parts)


def body(
    train_in,
    train_out,
    query_in,
    query_out,
    input_basis,
    output_basis,
    corrected,
    train_seq,
    query_order,
):
    n, size = lax.axis_size("seq"), lax.axis_size("eig")
    outer = n // INNER
    me, e = lax.axis_index("seq"), lax.axis_index("eig")
    xy, z = me % INNER, me // INNER
    where = jnp.stack([me, e]).astype(jnp.int32)
    share = TOK_DEV // size
    query_rows = query_in.shape[0]
    depth_out, cols = output_basis.shape
    cols_own = cols // INNER
    rows_own = corrected.shape[0]
    rows_in = rows_own * INNER
    per_core = input_basis.shape[1] // rows_in

    def to_planes(x, width):
        pieces = [
            lax.dynamic_slice(x, (e * share, (z ^ m) * width), (share, width))
            for m in range(outer)
        ]
        return pieces[:1] + [
            swap(pieces[m], "seq", m * INNER) for m in range(1, outer)
        ]

    def in_plane(pieces):
        return [pieces[0]] + [swap(pieces[r], "seq", r) for r in range(1, INNER)]

    small = jnp.concatenate(
        [
            query_in,
            query_out,
            train_seq.astype(BF16).reshape(query_rows, -1),
            (query_order % QUERIES).astype(BF16)[:, None],
        ],
        axis=1,
    )[None]

    def grow(x, b, axis):
        other = swap(x, "seq", 1 << b)
        upper = (me >> b) & 1 == 1
        return jnp.concatenate(
            [jnp.where(upper, other, x), jnp.where(upper, x, other)], axis=axis
        )

    for b in range(INNER.bit_length() - 1, n.bit_length() - 1):
        small = grow(small, b, 0)

    in_pieces = to_planes(train_in, rows_in)
    out_pieces = to_planes(after(train_out, *in_pieces[1:]), INNER * depth_out)

    basis_pieces = in_plane(
        split(
            where,
            [input_basis],
            [
                [
                    ((k * INNER + a) * rows_own, (k * INNER + a + 1) * rows_own)
                    for k in range(per_core)
                ]
                for a in range(INNER)
            ],
        )
    )

    small = small[:, None]
    for b in bits(INNER):
        small = grow(small, b, 1)
    small = small.reshape(n * query_rows, -1)
    din, dout = query_in.shape[1], query_out.shape[1]
    seq = small[:, din + dout : -1].reshape(n, 1, TOK_DEV).astype(F32)
    labels = small[:, -1].astype(F32)
    hot = (labels[:, None] == jnp.arange(QUERIES, dtype=F32)[None, :]).astype(F32)
    queries = small.shape[0]

    in_rel = after(jnp.stack(in_pieces), *basis_pieces[1:])
    in_rel = jnp.concatenate(in_plane([in_rel] * INNER))
    in_parts = [in_rel] + [swap(in_rel, "eig", m) for m in range(1, size)]

    quarter = [[(a * cols_own, (a + 1) * cols_own)] for a in range(INNER)]
    inverse = invert(in_plane(split(where, [after(corrected, in_rel)], quarter)))

    out_rel = jnp.concatenate(in_plane(split(where, out_pieces, [[(a * depth_out, (a + 1) * depth_out)] for a in range(INNER)])))
    out_parts = [out_rel] + [swap(out_rel, "eig", m) for m in range(1, size)]

    basis_in = unxor(jnp.concatenate(basis_pieces), xy).reshape(rows_in, -1).T
    query_rows_in = lax.dynamic_slice_in_dim(small, z * rows_in, rows_in, 1)
    query_rows_in = jnp.pad(query_rows_in, ((0, TOK_DEV - queries), (0, 0)))
    rotated = rotate_in(where, query_rows_in, basis_in, in_parts, n, per_core, outer)
    rotated = rotated.reshape(per_core, n + 1, size, rows_own // size, TOK_DEV)
    rotated = jnp.stack(
        [pick(rotated, e, 2)]
        + [swap(pick(rotated, e ^ m, 2), "eig", m) for m in range(1, size)]
    )
    rotated = unxor(rotated, e).reshape((outer,) + rotated.shape[2:])
    for b in bits(outer):
        bit = (z >> b) & 1
        pairs = rotated.reshape((-1, 2) + rotated.shape[1:])
        rotated = add(
            pick(pairs, bit, 1), swap(pick(pairs, 1 - bit, 1), "seq", INNER << b)
        )
    rotated = rotated[0]

    query_b = lax.dynamic_slice_in_dim(small, din + me * depth_out, depth_out, 1)
    query_b = jnp.dot(query_b, output_basis, preferred_element_type=F32).astype(BF16)
    for b in bits(n):
        query_b = add(query_b, swap(query_b, "seq", 1 << b))
    query_b = lax.dynamic_slice_in_dim(query_b, xy * cols_own, cols_own, 1)
    query_b = jnp.pad(query_b.astype(F32), ((0, TOK_DEV - queries), (0, 0))).T

    basis_out = output_basis.reshape(depth_out, INNER, cols_own).transpose(1, 2, 0)
    found = []
    for chunk in range(INNER):
        sx, kx, sy, ky = rotate_out(where, basis_out, out_parts, chunk, outer)
        if chunk > 0:
            sx, sy = after((sx, sy), rx, ry)
        if chunk == 2:
            sx, sy = after((sx, sy), a_parts[0])
        rx, ry = swap(sx, "seq", 1), swap(sy, "seq", 2)
        if chunk == 0:
            a_parts = jnp.stack(in_plane([after(rotated, rx, ry)] * INNER))
            a_parts = [a_parts] + [swap(a_parts, "eig", m) for m in range(1, size)]
            if a_parts[0].shape[2] % 16:
                whole = unxor(jnp.stack(a_parts), e).transpose(1, 2, 0, 3, 4)
                a_parts = [whole.reshape(INNER, n + 1, rows_own, TOK_DEV)]
        low = add(kx[0], rx[0], swap(add(kx[1], rx[1]), "seq", 2))
        high = add(ky[0], ry[0], swap(add(ky[1], ry[1]), "seq", 1))
        held = jnp.concatenate([low, high])
        if chunk == 0:
            held = after(held, rotated)
        for b in bits(outer):
            bit = (z >> b) & 1
            pairs = held.reshape((-1, 2) + held.shape[1:])
            held = add(
                pick(pairs, bit, 1), swap(pick(pairs, 1 - bit, 1), "seq", INNER << b)
            )
        masks = [0]
        scored = []
        for b in reversed(bits(outer)):
            other = swap(held, "seq", INNER << b)
            new = [m | (1 << b) for m in masks]
            if b == 0:
                scored.append((held, masks))
                scored.append((other, new))
            else:
                held = jnp.concatenate([held, other])
                masks = masks + new
        parts = []
        order = []
        for b_part, b_masks in scored:
            parts.append(
                score(
                    where, b_part, a_parts, inverse, query_b, seq, chunk, outer, b_masks
                )
            )
            order += b_masks
        parts = jnp.concatenate(parts)[:, :, :queries]
        parts = jnp.stack([parts[order.index(m)] for m in range(outer)])
        found.append(unxor(parts, z))
    per_token = jnp.concatenate(found)
    scores = jnp.sum(per_token[:, :, :, None] * hot[None, None], axis=2)
    scores = lax.all_to_all(scores, "seq", split_axis=0, concat_axis=0, tiled=True)
    scores = jnp.sum(scores, axis=0)
    for b in bits(size):
        scores = scores + swap(scores, "eig", 1 << b)
    factor = 1.0 / math.sqrt(DIN * EIGOUT * (TOK_DEV / SEQ_DEV) * (queries / QUERIES))
    return scores * factor


def solution(mesh):
    placed = (
        P("seq", None),
        P("seq", None),
        P("seq", None),
        P("seq", None),
        P("seq", "eig"),
        P("seq", "eig"),
        P("seq", "eig"),
        P("seq"),
        P("seq"),
    )
    return jax.shard_map(
        body, mesh=mesh, in_specs=placed, out_specs=P("seq", None), check_vma=False
    )
```

```python
import functools
import math

import jax
import jax.numpy as jnp
from jax import lax
from jax.experimental import pallas as pl
from jax.experimental.pallas import tpu as pltpu
from jax.sharding import PartitionSpec as P

DIN = 5120
EIGOUT = 6912
TOK_DEV = 128
SEQ_DEV = 2
QUERIES = 16
DAMPING = 0.1
INNER = 4
F32 = jnp.float32
BF16 = jnp.bfloat16
NT = (((1,), (1,)), ((), ()))
VMEM = pl.BlockSpec(memory_space=pltpu.VMEM)
SMEM = pl.BlockSpec(memory_space=pltpu.SMEM)


def bits(count):
    return range(count.bit_length() - 1)


def pick(x, index, axis=0):
    return lax.dynamic_index_in_dim(x, index, axis, keepdims=False)


def swap(x, axis, mask):
    size = lax.axis_size(axis)
    return lax.ppermute(x, axis, [(i, i ^ mask) for i in range(size)])


def unxor(x, index):
    size = x.shape[0]
    for b in bits(size):
        pairs = x.reshape((size >> (b + 1), 2, 1 << b) + x.shape[1:])
        turned = jnp.concatenate([pairs[:, 1:], pairs[:, :1]], axis=1)
        x = jnp.where((index >> b) & 1 == 1, turned, pairs).reshape(x.shape)
    return x


def after(x, *done):
    return lax.optimization_barrier((x,) + done)[0]


def add(*terms):
    total = terms[0].astype(F32)
    for term in terms[1:]:
        total = total + term.astype(F32)
    return total.astype(BF16)


EXTRA = 8


def padded(width):
    return -(-width // 128) * 128


def call(kernel, outs, *args, scratch=(), mib=40, flops=0):
    moved = sum(x.size * x.dtype.itemsize for x in list(args) + list(outs))
    return pl.pallas_call(
        kernel,
        out_shape=list(outs),
        in_specs=[SMEM] + [VMEM] * (len(args) - 1),
        out_specs=[VMEM] * len(outs),
        scratch_shapes=list(scratch),
        compiler_params=pltpu.CompilerParams(vmem_limit_bytes=mib << 20),
        cost_estimate=pl.CostEstimate(flops=flops, bytes_accessed=moved, transcendentals=0),
    )(*args)


def pack_kernel(widths, where, t_out, t_in, q_out, q_in, info, *outs):
    z, e = where[0] // INNER, where[1]
    share = outs[0].shape[0] - EXTRA
    rows = pl.ds(pl.multiple_of(e * share, 16), share)
    wide, narrow = widths
    for v in range(len(outs)):

        @pl.when(z == v)
        def _(v=v):
            for m, out in enumerate(outs):
                place = m ^ v
                for tokens, queries, width, at, last in (
                    (t_out, q_out, wide, 0, None),
                    (t_in, q_in, narrow, padded(wide), info),
                ):
                    cols = slice(place * width, (place + 1) * width)
                    out[:share, at : at + width] = tokens[rows, cols]
                    row = lax.broadcasted_iota(jnp.int32, (EXTRA, width), 0)
                    extra = jnp.zeros((EXTRA, width), F32)
                    count = queries.shape[0]
                    for i in range(count):
                        extra = jnp.where(row == i, queries[i : i + 1, cols].astype(F32), extra)
                    if last is not None:
                        extra = jnp.where(row == count, last[:, :width].astype(F32), extra)
                    out[share:, at : at + width] = extra.astype(BF16)


def pack(where, t_out, t_in, q_out, q_in, info, share, outer):
    wide, narrow = t_out.shape[1] // outer, t_in.shape[1] // outer
    shape = jax.ShapeDtypeStruct((share + EXTRA, padded(wide) + padded(narrow)), BF16)
    return call(
        functools.partial(pack_kernel, (wide, narrow)),
        [shape] * outer,
        where,
        t_out,
        t_in,
        q_out,
        q_in,
        info,
    )


def split_kernel(pieces, common, count, where, *refs):
    sources, outs = refs[:count], refs[count : count + len(pieces)]
    xy = where[0] % INNER
    if common:
        for s, source in enumerate(sources):
            refs[-1][s] = source[:, common[0] : common[1]]
    for v in range(INNER):

        @pl.when(xy == v)
        def _(v=v):
            for r, out in enumerate(outs):
                for start, stop, at in pieces[r ^ v]:
                    for s, source in enumerate(sources):
                        out[s, :, at : at + stop - start] = source[:, start:stop]


def split(where, sources, pieces, common=None):
    rows = sources[0].shape[0]
    width = max(at + stop - start for start, stop, at in pieces[0])
    outs = [jax.ShapeDtypeStruct((len(sources), rows, width), BF16)] * len(pieces)
    if common:
        outs.append(
            jax.ShapeDtypeStruct((len(sources), rows, common[1] - common[0]), BF16)
        )
    return call(
        functools.partial(split_kernel, pieces, common, len(sources)), outs, where, *sources
    )


def invert_kernel(where, *refs):
    sources, out = refs[:-1], refs[-1]
    rows = sources[0].shape[1]
    xy = where[0] % INNER
    for v in range(INNER):

        @pl.when(xy == v)
        def _(v=v):
            for r, source in enumerate(sources):
                damped = source[0].astype(F32) + DAMPING
                out[:, (r ^ v) * rows : ((r ^ v) + 1) * rows] = (1.0 / damped).T


def invert(where, sources):
    _, rows, cols = sources[0].shape
    shape = jax.ShapeDtypeStruct((cols, len(sources) * rows), F32)
    return call(invert_kernel, [shape], where, *sources)[0]


def gather_rows(parts, e, index, share, cols):
    shares = []
    for h in range(len(parts)):
        rows = parts[0][index, :share, cols]
        for m in range(1, len(parts)):
            rows = jnp.where((e ^ m) == h, parts[m][index, :share, cols], rows)
        shares.append(rows)
    return jnp.concatenate(shares, axis=0) if len(shares) > 1 else shares[0]


def grouped(refs):
    return [refs[i : i + INNER] for i in range(0, len(refs), INNER)]


def rotate_in_kernel(n, blocks, query_rows, at, where, *refs):
    pieces, refs = refs[:INNER], refs[INNER:]
    parts = refs[:-5]
    out, info, basis, rows, queries = refs[-5:]
    xy, z, e = where[0] % INNER, where[0] // INNER, where[1]
    depth = rows.shape[1]
    cols = slice(at, at + depth)
    width = basis.shape[0] // blocks
    share = TOK_DEV // len(parts)

    def store(group, product, lane):
        for k in range(blocks):
            out[k, group] = product[
                k * width : (k + 1) * width, lane * TOK_DEV : (lane + 1) * TOK_DEV
            ].astype(BF16)

    queries[...] = jnp.zeros_like(queries)
    for v in range(INNER):

        @pl.when(xy == v)
        def _(v=v):
            step = depth // INNER
            for r, piece in enumerate(pieces):
                place = (r ^ v) * step
                basis[:, place : place + step] = piece[0].astype(F32).T.astype(BF16)
            for g in range(n):
                place = ((g % INNER) ^ v) * (n // INNER) + ((g // INNER) ^ z)
                extra = parts[0][place, share:, cols].astype(F32)
                queries[g * query_rows : (g + 1) * query_rows] = extra[:query_rows]
                info[g] = extra[:, : info.shape[2]]

    store(
        n,
        lax.dot_general(
            basis[...], queries[...].astype(BF16), NT, preferred_element_type=F32
        ),
        0,
    )

    @pl.loop(0, n // INNER)
    def _(plane):
        for v in range(INNER):

            @pl.when(xy == v)
            def _(v=v):
                for p in range(INNER):
                    rows[p * TOK_DEV : (p + 1) * TOK_DEV] = gather_rows(
                        parts, e, (p ^ v) * (n // INNER) + (plane ^ z), share, cols
                    )

        product = lax.dot_general(basis[...], rows[...], NT, preferred_element_type=F32)
        for p in range(INNER):
            store(plane * INNER + p, product, p)


def rotate_in(where, pieces, parts, n, blocks, query_rows, at):
    _, width, cols = pieces[0].shape
    depth = INNER * width
    return call(
        functools.partial(rotate_in_kernel, n, blocks, query_rows, at),
        [
            jax.ShapeDtypeStruct((blocks, n + 1, cols // blocks, TOK_DEV), BF16),
            jax.ShapeDtypeStruct((n, EXTRA, 256), F32),
        ],
        where,
        *pieces,
        *parts,
        scratch=[
            pltpu.VMEM((cols, depth), BF16),
            pltpu.VMEM((INNER * TOK_DEV, depth), BF16),
            pltpu.VMEM((TOK_DEV, depth), F32),
        ],
        mib=48,
        flops=2 * (n + 1) * TOK_DEV * cols * depth,
    )


def rotate_out_kernel(chunk, outer, query_rows, where, basis, *refs):
    parts, outs = grouped(refs[:-6]), refs[-6:-2]
    rows, queries = refs[-2:]
    sx, kx, sy, ky = outs
    xy, z, e = where[0] % INNER, where[0] // INNER, where[1]
    half = outer // 2
    cols, depth = basis.shape[1], basis.shape[2]
    share = TOK_DEV // len(parts)
    total = queries.shape[0]

    for v in range(INNER):

        @pl.when((pl.program_id(0) == 0) & (xy == v))
        def _(v=v):
            for p in range(outer):
                group = chunk * outer + p
                rows[p * TOK_DEV : (p + 1) * TOK_DEV] = gather_rows(
                    [part[(p % INNER) ^ v] for part in parts],
                    e,
                    (group // INNER) ^ z,
                    share,
                    slice(0, depth),
                )
            if chunk == 0:
                for g in range(outer * INNER):
                    part = parts[0][(g % INNER) ^ v]
                    extra = part[(g // INNER) ^ z, share:, :depth].astype(F32)
                    queries[g * query_rows : (g + 1) * query_rows] = extra[:query_rows]

    product = lax.dot_general(basis[0], rows[...], NT, preferred_element_type=F32)

    def put(ref, place, first):
        for p in range(half):
            lane = (first + p) * TOK_DEV
            ref[place, p * cols : (p + 1) * cols] = product[:, lane : lane + TOK_DEV].astype(
                BF16
            )

    for r, (a, i, b, j) in enumerate(
        [(kx, 0, ky, 0), (sx, 0, ky, 1), (kx, 1, sy, 0), (sx, 1, sy, 1)]
    ):

        @pl.when(pl.program_id(0) == r)
        def _(a=a, i=i, b=b, j=j):
            put(a, i, 0)
            put(b, j, half)
            if chunk == 0:
                turned = lax.dot_general(
                    queries[...].astype(BF16), basis[0], NT, preferred_element_type=F32
                )
                rest = padded(cols) - cols
                if rest:
                    turned = jnp.concatenate([turned, jnp.zeros((total, rest), F32)], axis=1)
                for k in range(padded(cols) // 128):
                    start = half * cols + k * total
                    a[i, start : start + total] = turned[:, k * 128 : (k + 1) * 128].astype(
                        BF16
                    )


def rotate_out(where, *, basis, parts, chunk, outer, query_rows):
    _, cols, depth = basis.shape
    half = outer // 2
    total = outer * INNER * query_rows
    flat = [part for group in parts for part in group]
    extra = total * padded(cols) // 128 if chunk == 0 else 0
    first = jax.ShapeDtypeStruct((2, half * cols + extra, TOK_DEV), BF16)
    second = jax.ShapeDtypeStruct((2, half * cols, TOK_DEV), BF16)
    outs = [first, first, second, second]
    return pl.pallas_call(
        functools.partial(rotate_out_kernel, chunk, outer, query_rows),
        out_shape=outs,
        grid_spec=pltpu.PrefetchScalarGridSpec(
            num_scalar_prefetch=1,
            grid=(INNER,),
            in_specs=[pl.BlockSpec((1, cols, depth), lambda r, w: (r ^ (w[0] % INNER), 0, 0))]
            + [pl.BlockSpec(part.shape, lambda r, w: (0, 0, 0)) for part in flat],
            out_specs=[pl.BlockSpec(out.shape, lambda r, w: (0, 0, 0)) for out in outs],
            scratch_shapes=[
                pltpu.VMEM((outer * TOK_DEV, depth), BF16),
                pltpu.VMEM((total, depth), F32),
            ],
        ),
        compiler_params=pltpu.CompilerParams(vmem_limit_bytes=48 << 20),
        cost_estimate=pl.CostEstimate(
            flops=2 * outer * TOK_DEV * basis.size,
            bytes_accessed=2 * (basis.size + outer * TOK_DEV * (INNER * cols + depth)),
            transcendentals=0,
        ),
    )(where, basis, *flat)


def score_kernel(chunk, outer, masks, shares, info_row, where, b_ref, inverse, query_b, info, *refs):
    a_refs, q_refs, out, a_all = refs[:shares], refs[shares:-2], refs[-2], refs[-1]
    z, e = where[0] // INNER, where[1]
    rows, width = a_all.shape[1], a_refs[0].shape[2]
    tile = 256 if rows % 256 == 0 else 128

    def gather(sources, group, slot):
        for r in range(INNER):
            for h in range(shares):
                a = sources[0][r, group]
                for m in range(1, shares):
                    a = jnp.where((e ^ m) == h, sources[m][r, group], a)
                start = (r * shares + h) * width
                a_all[slot, start : start + width] = a

    gather(q_refs, 0, len(masks))
    for p, mask in enumerate(masks):
        place = z ^ mask
        gather(a_refs, place, p)
        seq = info[chunk * outer + place][info_row : info_row + 1, :TOK_DEV]
        for member in range(SEQ_DEV):
            b = jnp.where(seq == member, b_ref[p].astype(F32), 0.0).astype(BF16)
            total = jnp.zeros((b.shape[0], TOK_DEV), F32)
            for start in range(0, rows, tile):
                grad = lax.dot_general(
                    b, a_all[p, start : start + tile], NT, preferred_element_type=F32
                )
                scaled = (grad * inverse[:, start : start + tile]).astype(BF16)
                total = total + jnp.dot(
                    scaled,
                    a_all[len(masks), start : start + tile],
                    preferred_element_type=F32,
                )
            out[p, member : member + 1] = jnp.sum(total * query_b[...], axis=0, keepdims=True)


def score(where, b, a_parts, inverse, query_b, info, chunk, outer, masks, info_row):
    cols, rows = inverse.shape
    count = len(masks)
    _, groups, width, _ = a_parts[0].shape
    return pl.pallas_call(
        functools.partial(score_kernel, chunk, outer, masks, len(a_parts), info_row),
        out_shape=jax.ShapeDtypeStruct((count, SEQ_DEV, TOK_DEV), F32),
        grid=(1,),
        in_specs=[SMEM]
        + [VMEM] * 4
        + [pl.BlockSpec((INNER, outer, width, TOK_DEV), lambda i: (0, chunk, 0, 0))]
        * len(a_parts)
        + [pl.BlockSpec((INNER, 1, width, TOK_DEV), lambda i: (0, groups - 1, 0, 0))]
        * len(a_parts),
        out_specs=VMEM,
        scratch_shapes=[pltpu.VMEM((count + 1, rows, TOK_DEV), BF16)],
        compiler_params=pltpu.CompilerParams(vmem_limit_bytes=48 << 20),
        cost_estimate=pl.CostEstimate(
            flops=16 * count * SEQ_DEV * TOK_DEV * cols * rows,
            bytes_accessed=2 * (b.size + a_parts[0].size + 2 * inverse.size),
            transcendentals=0,
        ),
    )(where, b, inverse, query_b, info, *a_parts, *a_parts)


def body(
    train_in,
    train_out,
    query_in,
    query_out,
    input_basis,
    output_basis,
    corrected,
    train_seq,
    query_order,
):
    n, size = lax.axis_size("seq"), lax.axis_size("eig")
    outer = n // INNER
    me, e = lax.axis_index("seq"), lax.axis_index("eig")
    xy, z = me % INNER, me // INNER
    where = jnp.stack([me, e]).astype(jnp.int32)
    share = TOK_DEV // size
    query_rows = query_in.shape[0]
    queries = n * query_rows
    depth_out, cols = output_basis.shape
    cols_own = cols // INNER
    rows_own = corrected.shape[0]
    rows_in = rows_own * INNER
    per_core = input_basis.shape[1] // rows_in

    def in_plane(pieces):
        return [pieces[0]] + [swap(pieces[r], "seq", r) for r in range(1, INNER)]

    def in_turn(pieces, first, last):
        done = [swap(after(pieces[r], *first), "seq", r) for r in range(1, INNER - 1)]
        x = after(pieces[-1], *last, done[0])
        return [pieces[0]] + done + [swap(x, "seq", INNER - 1)]

    info = jnp.concatenate([train_seq, query_order % QUERIES]).astype(BF16)
    info = jnp.pad(info, (0, padded(rows_in) - info.shape[0]))[None]
    sent = pack(where, train_out, train_in, query_out, query_in, info, share, outer)
    sent = [sent[0]] + [swap(sent[m], "seq", m * INNER) for m in range(1, outer)]

    basis_pieces = in_turn(
        split(
            where,
            [after(input_basis, sent[0])],
            [
                [
                    (
                        (k * INNER + a) * rows_own,
                        (k * INNER + a + 1) * rows_own,
                        k * rows_own,
                    )
                    for k in range(per_core)
                ]
                for a in range(INNER)
            ],
        ),
        sent[1:2],
        sent[2:3],
    )

    inverse = invert(
        where,
        in_turn(
            split(
                where,
                [after(corrected, sent[0])],
                [[(a * cols_own, (a + 1) * cols_own, 0)] for a in range(INNER)],
            ),
            (),
            (),
        ),
    )

    wide = padded(INNER * depth_out)
    basis_out = output_basis.reshape(depth_out, INNER, cols_own).transpose(1, 2, 0)
    *out_pieces, in_piece = split(
        after(where, inverse, basis_out, *basis_pieces[1:]),
        sent,
        [[(a * depth_out, (a + 1) * depth_out, 0)] for a in range(INNER)],
        (wide, wide + rows_in),
    )

    out_pieces = in_plane(out_pieces)
    parts = [out_pieces] + [
        [swap(x, "eig", m) for x in out_pieces] for m in range(1, size)
    ]
    in_rel = in_plane([after(in_piece, *out_pieces[1:])] * INNER)
    rotate = functools.partial(
        rotate_out, basis=basis_out, parts=parts, outer=outer, query_rows=query_rows
    )

    def plane_sum(sx, kx, sy, ky):
        rx, ry = yield (sx, 1), (sy, 2)
        low, high = yield (add(kx[1], rx[1]), 2), (add(ky[1], ry[1]), 1)
        return add(kx[0], rx[0], low), add(ky[0], ry[0], high)

    def planes_sum(held):
        for b in bits(outer):
            bit = (z >> b) & 1
            pairs = held.reshape((-1, 2) + held.shape[1:])
            (got,) = yield ((pick(pairs, 1 - bit, 1), INNER << b),)
            held = add(pick(pairs, bit, 1), got)
        masks = [0]
        for b in reversed(bits(outer)):
            (got,) = yield ((held, INNER << b),)
            more = [m | (1 << b) for m in masks]
            halves = [(held, masks), (got, more)]
            held, masks = jnp.concatenate([held, got]), masks + more
        return halves

    def query_sum(held):
        for b in bits(outer):
            (got,) = yield ((held, INNER << b),)
            held = add(held, got)
        return held

    partial_sums = [rotate(where, chunk=0)]
    in_rel = jnp.concatenate([after(x, partial_sums[0][2]) for x in in_rel])
    in_parts = [in_rel] + [swap(in_rel, "eig", m) for m in range(1, size)]
    rotated, info = rotate_in(
        after(where, partial_sums[0][2]), basis_pieces, in_parts, n, per_core, query_rows, 0
    )
    rotated = rotated.reshape(per_core, n + 1, size, rows_own // size, TOK_DEV)
    rotated = jnp.stack(
        [pick(rotated, e, 2)]
        + [swap(pick(rotated, e ^ m, 2), "eig", m) for m in range(1, size)]
    )
    rotated = unxor(rotated, e).reshape((outer,) + rotated.shape[2:])
    across = [[INNER * i + a for i in range(outer)] for a in range(INNER)]
    inside = [[INNER * i + a for a in range(INNER)] for i in range(outer)]
    rotated = lax.psum_scatter(
        rotated, "seq", scatter_dimension=0, tiled=True, axis_index_groups=across
    )
    a_parts = lax.all_gather(rotated, "seq", axis=0, tiled=True, axis_index_groups=inside)
    a_parts = [a_parts] + [swap(a_parts, "eig", m) for m in range(1, size)]
    if a_parts[0].shape[2] % 16:
        whole = unxor(jnp.stack(a_parts), e).transpose(1, 2, 0, 3, 4)
        a_parts = [whole.reshape(INNER, n + 1, rows_own, TOK_DEV)]

    active = {("plane", 0): plane_sum(*partial_sums[0])}
    got, fence, found, scored = {}, [], {}, {}
    step, query_b = 0, None
    while active:
        sends = {}
        for key in list(active):
            if key[0] == "query" and step < INNER:
                continue
            try:
                sends[key] = active[key].send(got.get(key))
                continue
            except StopIteration as stop:
                value = stop.value
            kind, chunk = key
            del active[key]
            if kind == "plane":
                low, high = value
                if chunk == 0:
                    at = outer // 2 * cols_own
                    active["query", 0] = query_sum(low[at:])
                    low = low[:at]
                held = jnp.concatenate([low, high]).reshape(outer, cols_own, TOK_DEV)
                active["planes", chunk] = planes_sum(held)
                sends["planes", chunk] = active["planes", chunk].send(None)
            elif kind == "query":
                value = value.reshape(-1, queries, TOK_DEV).transpose(0, 2, 1)
                value = value.reshape(-1, queries)[:cols_own].astype(F32)
                query_b = jnp.pad(value, ((0, 0), (0, TOK_DEV - queries)))
            else:
                found[chunk] = value
        if 0 < step < INNER:
            begun = plane_sum(*partial_sums[step])
            active["plane", step] = begun
            sends["plane", step] = begun.send(None)
        if step == INNER + 2:
            fence = fence + a_parts
        got = {}
        for key, items in sends.items():
            got[key] = [swap(after(x, *fence), "seq", mask) for x, mask in items]
        if step + 1 < INNER:
            ready = fence if step else [info]
            partial_sums.append(rotate(after(where, *ready), chunk=step + 1))
        fence = [x for items in got.values() for x in items]
        for chunk in sorted(set(found) - set(scored)):
            halves = found[chunk]
            masks = [m for _, part in halves for m in part]
            if active:
                halves = [(jnp.concatenate([x for x, _ in halves]), masks)]
            values = [
                score(
                    where, x, a_parts, inverse, query_b, info, chunk, outer, part, query_rows
                )
                for x, part in halves
            ]
            fence = fence + values[:1]
            values = jnp.concatenate(values)[:, :, :queries]
            scored[chunk] = unxor(
                jnp.stack([values[masks.index(m)] for m in range(outer)]), z
            )
        step += 1
    labels = info[:, query_rows, TOK_DEV : TOK_DEV + query_rows].reshape(-1)
    hot = (labels[:, None] == jnp.arange(QUERIES, dtype=F32)[None, :]).astype(F32)
    per_token = jnp.concatenate([scored[chunk] for chunk in range(INNER)])
    scores = jnp.sum(per_token[:, :, :, None] * hot[None, None], axis=2)
    scores = lax.all_to_all(scores, "seq", split_axis=0, concat_axis=0, tiled=True)
    scores = jnp.sum(scores, axis=0)
    for b in bits(size):
        scores = scores + swap(scores, "eig", 1 << b)
    factor = 1.0 / math.sqrt(DIN * EIGOUT * (TOK_DEV / SEQ_DEV) * (queries / QUERIES))
    return scores * factor


def solution(mesh):
    placed = (
        P("seq", None),
        P("seq", None),
        P("seq", None),
        P("seq", None),
        P("seq", "eig"),
        P("seq", "eig"),
        P("seq", "eig"),
        P("seq"),
        P("seq"),
    )
    return jax.shard_map(
        body, mesh=mesh, in_specs=placed, out_specs=P("seq", None), check_vma=False
    )
```

```python
import functools
import math

import jax
import jax.numpy as jnp
from jax import lax
from jax.experimental import pallas as pl
from jax.experimental.pallas import tpu as pltpu
from jax.sharding import PartitionSpec as P

DIN = 5120
EIGOUT = 6912
TOK_DEV = 128
SEQ_DEV = 2
QUERIES = 16
DAMPING = 0.1
INNER = 4
F32 = jnp.float32
BF16 = jnp.bfloat16
NT = (((1,), (1,)), ((), ()))
VMEM = pl.BlockSpec(memory_space=pltpu.VMEM)
SMEM = pl.BlockSpec(memory_space=pltpu.SMEM)


def bits(count):
    return range(count.bit_length() - 1)


def pick(x, index, axis=0):
    return lax.dynamic_index_in_dim(x, index, axis, keepdims=False)


def swap(x, axis, mask):
    size = lax.axis_size(axis)
    return lax.ppermute(x, axis, [(i, i ^ mask) for i in range(size)])


def unxor(x, index):
    size = x.shape[0]
    for b in bits(size):
        pairs = x.reshape((size >> (b + 1), 2, 1 << b) + x.shape[1:])
        turned = jnp.concatenate([pairs[:, 1:], pairs[:, :1]], axis=1)
        x = jnp.where((index >> b) & 1 == 1, turned, pairs).reshape(x.shape)
    return x


def after(x, *done):
    return lax.optimization_barrier((x,) + done)[0]


def add(*terms):
    total = terms[0].astype(F32)
    for term in terms[1:]:
        total = total + term.astype(F32)
    return total.astype(BF16)


EXTRA = 8


def padded(width):
    return -(-width // 128) * 128


def call(kernel, outs, *args, scratch=(), mib=40, flops=0):
    moved = sum(x.size * x.dtype.itemsize for x in list(args) + list(outs))
    return pl.pallas_call(
        kernel,
        out_shape=list(outs),
        in_specs=[SMEM] + [VMEM] * (len(args) - 1),
        out_specs=[VMEM] * len(outs),
        scratch_shapes=list(scratch),
        compiler_params=pltpu.CompilerParams(vmem_limit_bytes=mib << 20),
        cost_estimate=pl.CostEstimate(flops=flops, bytes_accessed=moved, transcendentals=0),
    )(*args)


def pack_kernel(widths, where, t_out, t_in, q_out, q_in, info, *outs):
    z, e = where[0] // INNER, where[1]
    share = outs[0].shape[0] - EXTRA
    rows = pl.ds(pl.multiple_of(e * share, 16), share)
    wide, narrow = widths
    for v in range(len(outs)):

        @pl.when(z == v)
        def _(v=v):
            for m, out in enumerate(outs):
                place = m ^ v
                for tokens, queries, width, at, last in (
                    (t_out, q_out, wide, 0, None),
                    (t_in, q_in, narrow, padded(wide), info),
                ):
                    cols = slice(place * width, (place + 1) * width)
                    out[:share, at : at + width] = tokens[rows, cols]
                    row = lax.broadcasted_iota(jnp.int32, (EXTRA, width), 0)
                    extra = jnp.zeros((EXTRA, width), F32)
                    count = queries.shape[0]
                    for i in range(count):
                        extra = jnp.where(row == i, queries[i : i + 1, cols].astype(F32), extra)
                    if last is not None:
                        extra = jnp.where(row == count, last[:, :width].astype(F32), extra)
                    out[share:, at : at + width] = extra.astype(BF16)


def pack(where, t_out, t_in, q_out, q_in, info, share, outer):
    wide, narrow = t_out.shape[1] // outer, t_in.shape[1] // outer
    shape = jax.ShapeDtypeStruct((share + EXTRA, padded(wide) + padded(narrow)), BF16)
    return call(
        functools.partial(pack_kernel, (wide, narrow)),
        [shape] * outer,
        where,
        t_out,
        t_in,
        q_out,
        q_in,
        info,
    )


def split_kernel(pieces, common, count, where, *refs):
    sources, outs = refs[:count], refs[count : count + len(pieces)]
    xy = where[0] % INNER
    if common:
        for s, source in enumerate(sources):
            refs[-1][s] = source[:, common[0] : common[1]]
    for v in range(INNER):

        @pl.when(xy == v)
        def _(v=v):
            for r, out in enumerate(outs):
                for start, stop, at in pieces[r ^ v]:
                    for s, source in enumerate(sources):
                        out[s, :, at : at + stop - start] = source[:, start:stop]


def split(where, sources, pieces, common=None):
    rows = sources[0].shape[0]
    width = max(at + stop - start for start, stop, at in pieces[0])
    outs = [jax.ShapeDtypeStruct((len(sources), rows, width), BF16)] * len(pieces)
    if common:
        outs.append(
            jax.ShapeDtypeStruct((len(sources), rows, common[1] - common[0]), BF16)
        )
    return call(
        functools.partial(split_kernel, pieces, common, len(sources)), outs, where, *sources
    )


def invert_kernel(where, *refs):
    sources, out = refs[:-1], refs[-1]
    rows = sources[0].shape[1]
    xy = where[0] % INNER
    for v in range(INNER):

        @pl.when(xy == v)
        def _(v=v):
            for r, source in enumerate(sources):
                damped = source[0].astype(F32) + DAMPING
                out[:, (r ^ v) * rows : ((r ^ v) + 1) * rows] = (1.0 / damped).T


def invert(where, sources):
    _, rows, cols = sources[0].shape
    shape = jax.ShapeDtypeStruct((cols, len(sources) * rows), F32)
    return call(invert_kernel, [shape], where, *sources)[0]


def gather_rows(parts, e, index, share, cols):
    shares = []
    for h in range(len(parts)):
        rows = parts[0][index, :share, cols]
        for m in range(1, len(parts)):
            rows = jnp.where((e ^ m) == h, parts[m][index, :share, cols], rows)
        shares.append(rows)
    return jnp.concatenate(shares, axis=0) if len(shares) > 1 else shares[0]


def grouped(refs):
    return [refs[i : i + INNER] for i in range(0, len(refs), INNER)]


def rotate_in_kernel(n, blocks, query_rows, at, where, *refs):
    pieces, refs = refs[:INNER], refs[INNER:]
    parts = refs[:-5]
    out, info, basis, rows, queries = refs[-5:]
    xy, z, e = where[0] % INNER, where[0] // INNER, where[1]
    depth = rows.shape[1]
    cols = slice(at, at + depth)
    width = basis.shape[0] // blocks
    share = TOK_DEV // len(parts)

    def store(group, product, lane):
        for k in range(blocks):
            out[k, group] = product[
                k * width : (k + 1) * width, lane * TOK_DEV : (lane + 1) * TOK_DEV
            ].astype(BF16)

    queries[...] = jnp.zeros_like(queries)
    for v in range(INNER):

        @pl.when(xy == v)
        def _(v=v):
            step = depth // INNER
            for r, piece in enumerate(pieces):
                place = (r ^ v) * step
                basis[:, place : place + step] = piece[0].astype(F32).T.astype(BF16)
            for g in range(n):
                place = ((g % INNER) ^ v) * (n // INNER) + ((g // INNER) ^ z)
                extra = parts[0][place, share:, cols].astype(F32)
                queries[g * query_rows : (g + 1) * query_rows] = extra[:query_rows]
                info[g] = extra[:, : info.shape[2]]

    store(
        n,
        lax.dot_general(
            basis[...], queries[...].astype(BF16), NT, preferred_element_type=F32
        ),
        0,
    )

    @pl.loop(0, n // INNER)
    def _(plane):
        for v in range(INNER):

            @pl.when(xy == v)
            def _(v=v):
                for p in range(INNER):
                    rows[p * TOK_DEV : (p + 1) * TOK_DEV] = gather_rows(
                        parts, e, (p ^ v) * (n // INNER) + (plane ^ z), share, cols
                    )

        product = lax.dot_general(basis[...], rows[...], NT, preferred_element_type=F32)
        for p in range(INNER):
            store(plane * INNER + p, product, p)


def rotate_in(where, pieces, parts, n, blocks, query_rows, at):
    _, width, cols = pieces[0].shape
    depth = INNER * width
    return call(
        functools.partial(rotate_in_kernel, n, blocks, query_rows, at),
        [
            jax.ShapeDtypeStruct((blocks, n + 1, cols // blocks, TOK_DEV), BF16),
            jax.ShapeDtypeStruct((n, EXTRA, 256), F32),
        ],
        where,
        *pieces,
        *parts,
        scratch=[
            pltpu.VMEM((cols, depth), BF16),
            pltpu.VMEM((INNER * TOK_DEV, depth), BF16),
            pltpu.VMEM((TOK_DEV, depth), F32),
        ],
        mib=48,
        flops=2 * (n + 1) * TOK_DEV * cols * depth,
    )


def rotate_out_kernel(chunk, outer, query_rows, where, basis, *refs):
    parts, outs = grouped(refs[:-6]), refs[-6:-2]
    rows, queries = refs[-2:]
    sx, kx, sy, ky = outs
    xy, z, e = where[0] % INNER, where[0] // INNER, where[1]
    half = outer // 2
    cols, depth = basis.shape[1], basis.shape[2]
    share = TOK_DEV // len(parts)
    total = queries.shape[0]

    for v in range(INNER):

        @pl.when((pl.program_id(0) == 0) & (xy == v))
        def _(v=v):
            for p in range(outer):
                group = chunk * outer + p
                rows[p * TOK_DEV : (p + 1) * TOK_DEV] = gather_rows(
                    [part[(p % INNER) ^ v] for part in parts],
                    e,
                    (group // INNER) ^ z,
                    share,
                    slice(0, depth),
                )
            if chunk == 0:
                for g in range(outer * INNER):
                    part = parts[0][(g % INNER) ^ v]
                    extra = part[(g // INNER) ^ z, share:, :depth].astype(F32)
                    queries[g * query_rows : (g + 1) * query_rows] = extra[:query_rows]

    product = lax.dot_general(basis[0], rows[...], NT, preferred_element_type=F32)

    def put(ref, place, first):
        for p in range(half):
            lane = (first + p) * TOK_DEV
            ref[place, p * cols : (p + 1) * cols] = product[:, lane : lane + TOK_DEV].astype(
                BF16
            )

    for r, (a, i, b, j) in enumerate(
        [(kx, 0, ky, 0), (sx, 0, ky, 1), (kx, 1, sy, 0), (sx, 1, sy, 1)]
    ):

        @pl.when(pl.program_id(0) == r)
        def _(a=a, i=i, b=b, j=j):
            put(a, i, 0)
            put(b, j, half)
            if chunk == 0:
                turned = lax.dot_general(
                    queries[...].astype(BF16), basis[0], NT, preferred_element_type=F32
                )
                rest = padded(cols) - cols
                if rest:
                    turned = jnp.concatenate([turned, jnp.zeros((total, rest), F32)], axis=1)
                for k in range(padded(cols) // 128):
                    start = half * cols + k * total
                    a[i, start : start + total] = turned[:, k * 128 : (k + 1) * 128].astype(
                        BF16
                    )


def rotate_out(where, *, basis, parts, chunk, outer, query_rows):
    _, cols, depth = basis.shape
    half = outer // 2
    total = outer * INNER * query_rows
    flat = [part for group in parts for part in group]
    extra = total * padded(cols) // 128 if chunk == 0 else 0
    first = jax.ShapeDtypeStruct((2, half * cols + extra, TOK_DEV), BF16)
    second = jax.ShapeDtypeStruct((2, half * cols, TOK_DEV), BF16)
    outs = [first, first, second, second]
    return pl.pallas_call(
        functools.partial(rotate_out_kernel, chunk, outer, query_rows),
        out_shape=outs,
        grid_spec=pltpu.PrefetchScalarGridSpec(
            num_scalar_prefetch=1,
            grid=(INNER,),
            in_specs=[pl.BlockSpec((1, cols, depth), lambda r, w: (r ^ (w[0] % INNER), 0, 0))]
            + [pl.BlockSpec(part.shape, lambda r, w: (0, 0, 0)) for part in flat],
            out_specs=[pl.BlockSpec(out.shape, lambda r, w: (0, 0, 0)) for out in outs],
            scratch_shapes=[
                pltpu.VMEM((outer * TOK_DEV, depth), BF16),
                pltpu.VMEM((total, depth), F32),
            ],
        ),
        compiler_params=pltpu.CompilerParams(vmem_limit_bytes=48 << 20),
        cost_estimate=pl.CostEstimate(
            flops=2 * outer * TOK_DEV * basis.size,
            bytes_accessed=2 * (basis.size + outer * TOK_DEV * (INNER * cols + depth)),
            transcendentals=0,
        ),
    )(where, basis, *flat)


def score_kernel(chunk, outer, masks, shares, info_row, where, b_ref, inverse, query_b, info, *refs):
    a_refs, q_refs, out, a_all = refs[:shares], refs[shares:-2], refs[-2], refs[-1]
    z, e = where[0] // INNER, where[1]
    rows, width = a_all.shape[1], a_refs[0].shape[2]
    tile = 256 if rows % 256 == 0 else 128

    def gather(sources, group, slot):
        for r in range(INNER):
            for h in range(shares):
                a = sources[0][r, group]
                for m in range(1, shares):
                    a = jnp.where((e ^ m) == h, sources[m][r, group], a)
                start = (r * shares + h) * width
                a_all[slot, start : start + width] = a

    gather(q_refs, 0, len(masks))
    for p, mask in enumerate(masks):
        place = z ^ mask
        gather(a_refs, place, p)
        seq = info[chunk * outer + place][info_row : info_row + 1, :TOK_DEV]
        for member in range(SEQ_DEV):
            b = jnp.where(seq == member, b_ref[p].astype(F32), 0.0).astype(BF16)
            total = jnp.zeros((b.shape[0], TOK_DEV), F32)
            for start in range(0, rows, tile):
                grad = lax.dot_general(
                    b, a_all[p, start : start + tile], NT, preferred_element_type=F32
                )
                scaled = (grad * inverse[:, start : start + tile]).astype(BF16)
                total = total + jnp.dot(
                    scaled,
                    a_all[len(masks), start : start + tile],
                    preferred_element_type=F32,
                )
            out[p, member : member + 1] = jnp.sum(total * query_b[...], axis=0, keepdims=True)


def score(where, b, a_parts, inverse, query_b, info, chunk, outer, masks, info_row):
    cols, rows = inverse.shape
    count = len(masks)
    _, groups, width, _ = a_parts[0].shape
    return pl.pallas_call(
        functools.partial(score_kernel, chunk, outer, masks, len(a_parts), info_row),
        out_shape=jax.ShapeDtypeStruct((count, SEQ_DEV, TOK_DEV), F32),
        grid=(1,),
        in_specs=[SMEM]
        + [VMEM] * 4
        + [pl.BlockSpec((INNER, outer, width, TOK_DEV), lambda i: (0, chunk, 0, 0))]
        * len(a_parts)
        + [pl.BlockSpec((INNER, 1, width, TOK_DEV), lambda i: (0, groups - 1, 0, 0))]
        * len(a_parts),
        out_specs=VMEM,
        scratch_shapes=[pltpu.VMEM((count + 1, rows, TOK_DEV), BF16)],
        compiler_params=pltpu.CompilerParams(vmem_limit_bytes=48 << 20),
        cost_estimate=pl.CostEstimate(
            flops=16 * count * SEQ_DEV * TOK_DEV * cols * rows,
            bytes_accessed=2 * (b.size + a_parts[0].size + 2 * inverse.size),
            transcendentals=0,
        ),
    )(where, b, inverse, query_b, info, *a_parts, *a_parts)


def body(
    train_in,
    train_out,
    query_in,
    query_out,
    input_basis,
    output_basis,
    corrected,
    train_seq,
    query_order,
):
    n, size = lax.axis_size("seq"), lax.axis_size("eig")
    outer = n // INNER
    me, e = lax.axis_index("seq"), lax.axis_index("eig")
    xy, z = me % INNER, me // INNER
    where = jnp.stack([me, e]).astype(jnp.int32)
    share = TOK_DEV // size
    query_rows = query_in.shape[0]
    queries = n * query_rows
    depth_out, cols = output_basis.shape
    cols_own = cols // INNER
    rows_own = corrected.shape[0]
    rows_in = rows_own * INNER
    per_core = input_basis.shape[1] // rows_in

    def in_plane(pieces):
        return [pieces[0]] + [swap(pieces[r], "seq", r) for r in range(1, INNER)]

    def in_turn(pieces, first, last):
        done = [swap(after(pieces[r], *first), "seq", r) for r in range(1, INNER - 1)]
        x = after(pieces[-1], *last, done[0])
        return [pieces[0]] + done + [swap(x, "seq", INNER - 1)]

    info = jnp.concatenate([train_seq, query_order % QUERIES]).astype(BF16)
    info = jnp.pad(info, (0, padded(rows_in) - info.shape[0]))[None]
    sent = pack(where, train_out, train_in, query_out, query_in, info, share, outer)
    sent = [sent[0]] + [swap(sent[m], "seq", m * INNER) for m in range(1, outer)]

    basis_pieces = in_turn(
        split(
            where,
            [after(input_basis, sent[0])],
            [
                [
                    (
                        (k * INNER + a) * rows_own,
                        (k * INNER + a + 1) * rows_own,
                        k * rows_own,
                    )
                    for k in range(per_core)
                ]
                for a in range(INNER)
            ],
        ),
        sent[1:2],
        sent[2:],
    )

    inverse = invert(
        where,
        in_turn(
            split(
                where,
                [after(corrected, sent[0])],
                [[(a * cols_own, (a + 1) * cols_own, 0)] for a in range(INNER)],
            ),
            (),
            (),
        ),
    )

    wide = padded(INNER * depth_out)
    basis_out = output_basis.reshape(depth_out, INNER, cols_own).transpose(1, 2, 0)
    *out_pieces, in_piece = split(
        after(where, inverse, basis_out, *basis_pieces[1:-1]),
        sent,
        [[(a * depth_out, (a + 1) * depth_out, 0)] for a in range(INNER)],
        (wide, wide + rows_in),
    )

    out_pieces = in_plane(out_pieces)
    parts = [out_pieces] + [
        [swap(x, "eig", m) for x in out_pieces] for m in range(1, size)
    ]
    in_rel = in_plane([after(in_piece, *out_pieces[1:], basis_pieces[-1])] * INNER)
    rotate = functools.partial(
        rotate_out, basis=basis_out, parts=parts, outer=outer, query_rows=query_rows
    )

    def plane_sum(sx, kx, sy, ky):
        rx, ry = yield (sx, 1), (sy, 2)
        low, high = yield (add(kx[1], rx[1]), 2), (add(ky[1], ry[1]), 1)
        return add(kx[0], rx[0], low), add(ky[0], ry[0], high)

    def planes_sum(held, extra=None):
        for b in bits(outer):
            bit = (z >> b) & 1
            pairs = held.reshape((-1, 2) + held.shape[1:])
            x = pick(pairs, 1 - bit, 1)
            if extra is not None:
                x = jnp.concatenate([x.reshape(-1, TOK_DEV), extra])
            (got,) = yield ((x, INNER << b),)
            if extra is not None:
                at = got.shape[0] - extra.shape[0]
                extra = add(extra, got[at:])
                got = got[:at].reshape((-1,) + held.shape[1:])
            held = add(pick(pairs, bit, 1), got)
        masks = [0]
        for b in reversed(bits(outer)):
            shape = held.shape
            flat = held.reshape(-1, TOK_DEV)
            items = [flat] if b else [flat[:16], flat[16:]]
            got = yield tuple((x, INNER << b) for x in items)
            more = [m | (1 << b) for m in masks]
            held, masks = jnp.concatenate([flat] + got), masks + more
            held = held.reshape((2 * shape[0],) + shape[1:])
        return held, masks, extra

    partial_sums = [rotate(where, chunk=0)]
    partial_sums.append(rotate(after(where, partial_sums[0][2]), chunk=1))
    in_rel = jnp.concatenate([after(x, partial_sums[0][2]) for x in in_rel])
    in_parts = [in_rel] + [swap(in_rel, "eig", m) for m in range(1, size)]
    rotated, info = rotate_in(
        after(where, partial_sums[1][2]), basis_pieces, in_parts, n, per_core, query_rows, 0
    )
    rotated = rotated.reshape(per_core, n + 1, size, rows_own // size, TOK_DEV)
    swapped = [swap(pick(rotated, e ^ m, 2), "eig", m) for m in range(1, size)]
    rotated = jnp.stack([pick(rotated, e, 2)] + swapped)
    rotated = unxor(rotated, e).reshape((outer,) + rotated.shape[2:])
    across = [[INNER * i + a for i in range(outer)] for a in range(INNER)]
    inside = [[INNER * i + a for a in range(INNER)] for i in range(outer)]
    rotated = lax.psum_scatter(
        rotated, "seq", scatter_dimension=0, tiled=True, axis_index_groups=across
    )

    def between_cores(x):
        a_parts = [x] + [swap(x, "eig", m) for m in range(1, size)]
        if a_parts[0].shape[2] % 16:
            whole = unxor(jnp.stack(a_parts), e).transpose(1, 2, 0, 3, 4)
            a_parts = [whole.reshape(INNER, n + 1, rows_own, TOK_DEV)]
        return a_parts

    active = {("plane", 0): plane_sum(*partial_sums[0])}
    got, fence, found, scored = {}, [], {}, {}
    step, query_b = 0, None
    while active:
        sends = {}
        for key in list(active):
            try:
                sends[key] = active[key].send(got.get(key))
                continue
            except StopIteration as stop:
                value = stop.value
            kind, chunk = key
            del active[key]
            if kind == "plane":
                low, high = value
                at = outer // 2 * cols_own
                held = jnp.concatenate([low[:at], high]).reshape(outer, cols_own, TOK_DEV)
                active["planes", chunk] = planes_sum(held, None if chunk else low[at:])
                sends["planes", chunk] = active["planes", chunk].send(None)
            else:
                found[chunk] = value[:2]
                if chunk == 0:
                    value = value[2].reshape(-1, queries, TOK_DEV).transpose(0, 2, 1)
                    value = value.reshape(-1, queries)[:cols_own].astype(F32)
                    query_b = jnp.pad(value, ((0, 0), (0, TOK_DEV - queries)))
        if 0 < step < INNER:
            begun = plane_sum(*partial_sums[step])
            active["plane", step] = begun
            sends["plane", step] = begun.send(None)
        if step == 2:
            fence = fence + swapped
        if step == INNER:
            gathered = lax.all_gather(
                after(rotated, *fence), "seq", axis=0, tiled=True, axis_index_groups=inside
            )
        if step == INNER + 2:
            a_parts = between_cores(after(gathered, *fence))
            fence = fence + list(a_parts)
        if 0 < step < INNER:
            fence = fence + [partial_sums[step][2]]
        got = {}
        for key, items in sends.items():
            got[key] = [swap(after(x, *fence), "seq", mask) for x, mask in items]
        if 0 < step < INNER - 1:
            partial_sums.append(rotate(after(where, *fence), chunk=step + 1))
        fence = [x for items in got.values() for x in items]
        for chunk in sorted(set(found) - set(scored)):
            held, masks = found[chunk]
            here = where
            if len(fence) > 1:
                here = after(where, min(fence, key=lambda x: x.size))
            values = score(
                here, held, a_parts, inverse, query_b, info, chunk, outer, masks, query_rows
            )
            if chunk == 0:
                fence = fence + [values]
            values = values[:, :, :queries]
            scored[chunk] = unxor(
                jnp.stack([values[masks.index(m)] for m in range(outer)]), z
            )
        step += 1
    labels = info[:, query_rows, TOK_DEV : TOK_DEV + query_rows].reshape(-1)
    hot = (labels[:, None] == jnp.arange(QUERIES, dtype=F32)[None, :]).astype(F32)
    per_token = jnp.concatenate([scored[chunk] for chunk in range(INNER)])
    scores = jnp.sum(per_token[:, :, :, None] * hot[None, None], axis=2)
    scores = lax.all_to_all(scores, "seq", split_axis=0, concat_axis=0, tiled=True)
    scores = jnp.sum(scores, axis=0)
    for b in bits(size):
        scores = scores + swap(scores, "eig", 1 << b)
    factor = 1.0 / math.sqrt(DIN * EIGOUT * (TOK_DEV / SEQ_DEV) * (queries / QUERIES))
    return scores * factor


def solution(mesh):
    placed = (
        P("seq", None),
        P("seq", None),
        P("seq", None),
        P("seq", None),
        P("seq", "eig"),
        P("seq", "eig"),
        P("seq", "eig"),
        P("seq"),
        P("seq"),
    )
    return jax.shard_map(
        body, mesh=mesh, in_specs=placed, out_specs=P("seq", None), check_vma=False
    )
```

```python
import functools
import math

import jax
import jax.numpy as jnp
from jax import lax
from jax.experimental import pallas as pl
from jax.experimental.pallas import tpu as pltpu
from jax.sharding import PartitionSpec as P

DIN = 5120
EIGOUT = 6912
TOK_DEV = 128
SEQ_DEV = 2
QUERIES = 16
DAMPING = 0.1
INNER = 4
F32 = jnp.float32
BF16 = jnp.bfloat16
NT = (((1,), (1,)), ((), ()))
VMEM = pl.BlockSpec(memory_space=pltpu.VMEM)
SMEM = pl.BlockSpec(memory_space=pltpu.SMEM)


def bits(count):
    return range(count.bit_length() - 1)


def pick(x, index, axis=0):
    return lax.dynamic_index_in_dim(x, index, axis, keepdims=False)


def swap(x, axis, mask):
    size = lax.axis_size(axis)
    return lax.ppermute(x, axis, [(i, i ^ mask) for i in range(size)])


def unxor(x, index):
    size = x.shape[0]
    for b in bits(size):
        pairs = x.reshape((size >> (b + 1), 2, 1 << b) + x.shape[1:])
        turned = jnp.concatenate([pairs[:, 1:], pairs[:, :1]], axis=1)
        x = jnp.where((index >> b) & 1 == 1, turned, pairs).reshape(x.shape)
    return x


def after(x, *done):
    return lax.optimization_barrier((x,) + done)[0]


def add(*terms):
    total = terms[0].astype(F32)
    for term in terms[1:]:
        total = total + term.astype(F32)
    return total.astype(BF16)


EXTRA = 8


def padded(width):
    return -(-width // 128) * 128


def call(kernel, outs, *args, scratch=(), mib=40, flops=0):
    moved = sum(x.size * x.dtype.itemsize for x in list(args) + list(outs))
    return pl.pallas_call(
        kernel,
        out_shape=list(outs),
        in_specs=[SMEM] + [VMEM] * (len(args) - 1),
        out_specs=[VMEM] * len(outs),
        scratch_shapes=list(scratch),
        compiler_params=pltpu.CompilerParams(vmem_limit_bytes=mib << 20),
        cost_estimate=pl.CostEstimate(flops=flops, bytes_accessed=moved, transcendentals=0),
    )(*args)


def pack_kernel(widths, where, t_out, t_in, q_out, q_in, info, *outs):
    z, e = where[0] // INNER, where[1]
    share = outs[0].shape[0] - EXTRA
    rows = pl.ds(pl.multiple_of(e * share, 16), share)
    wide, narrow = widths
    for v in range(len(outs)):

        @pl.when(z == v)
        def _(v=v):
            for m, out in enumerate(outs):
                place = m ^ v
                for tokens, queries, width, at, last in (
                    (t_out, q_out, wide, 0, None),
                    (t_in, q_in, narrow, padded(wide), info),
                ):
                    cols = slice(place * width, (place + 1) * width)
                    out[:share, at : at + width] = tokens[rows, cols]
                    row = lax.broadcasted_iota(jnp.int32, (EXTRA, width), 0)
                    extra = jnp.zeros((EXTRA, width), F32)
                    count = queries.shape[0]
                    for i in range(count):
                        extra = jnp.where(row == i, queries[i : i + 1, cols].astype(F32), extra)
                    if last is not None:
                        extra = jnp.where(row == count, last[:, :width].astype(F32), extra)
                    out[share:, at : at + width] = extra.astype(BF16)


def pack(where, t_out, t_in, q_out, q_in, info, share, outer):
    wide, narrow = t_out.shape[1] // outer, t_in.shape[1] // outer
    shape = jax.ShapeDtypeStruct((share + EXTRA, padded(wide) + padded(narrow)), BF16)
    return call(
        functools.partial(pack_kernel, (wide, narrow)),
        [shape] * outer,
        where,
        t_out,
        t_in,
        q_out,
        q_in,
        info,
    )


def split_kernel(pieces, common, count, where, *refs):
    sources, outs = refs[:count], refs[count : count + len(pieces)]
    xy = where[0] % INNER
    if common:
        for s, source in enumerate(sources):
            refs[-1][s] = source[:, common[0] : common[1]]
    for v in range(INNER):

        @pl.when(xy == v)
        def _(v=v):
            for r, out in enumerate(outs):
                for start, stop, at in pieces[r ^ v]:
                    for s, source in enumerate(sources):
                        out[s, :, at : at + stop - start] = source[:, start:stop]


def split(where, sources, pieces, common=None):
    rows = sources[0].shape[0]
    width = max(at + stop - start for start, stop, at in pieces[0])
    outs = [jax.ShapeDtypeStruct((len(sources), rows, width), BF16)] * len(pieces)
    if common:
        outs.append(
            jax.ShapeDtypeStruct((len(sources), rows, common[1] - common[0]), BF16)
        )
    return call(
        functools.partial(split_kernel, pieces, common, len(sources)), outs, where, *sources
    )


def invert_kernel(where, *refs):
    sources, out = refs[:-1], refs[-1]
    rows = sources[0].shape[1]
    xy = where[0] % INNER
    for v in range(INNER):

        @pl.when(xy == v)
        def _(v=v):
            for r, source in enumerate(sources):
                damped = source[0].astype(F32) + DAMPING
                out[:, (r ^ v) * rows : ((r ^ v) + 1) * rows] = (1.0 / damped).T


def invert(where, sources):
    _, rows, cols = sources[0].shape
    shape = jax.ShapeDtypeStruct((cols, len(sources) * rows), F32)
    return call(invert_kernel, [shape], where, *sources)[0]


def gather_rows(parts, e, index, share, cols):
    shares = []
    for h in range(len(parts)):
        rows = parts[0][index, :share, cols]
        for m in range(1, len(parts)):
            rows = jnp.where((e ^ m) == h, parts[m][index, :share, cols], rows)
        shares.append(rows)
    return jnp.concatenate(shares, axis=0) if len(shares) > 1 else shares[0]


def grouped(refs):
    return [refs[i : i + INNER] for i in range(0, len(refs), INNER)]


def rotate_in_kernel(n, blocks, query_rows, at, where, *refs):
    pieces, refs = refs[:INNER], refs[INNER:]
    parts = refs[:-5]
    out, info, basis, rows, queries = refs[-5:]
    xy, z, e = where[0] % INNER, where[0] // INNER, where[1]
    depth = rows.shape[1]
    cols = slice(at, at + depth)
    width = basis.shape[0] // blocks
    share = TOK_DEV // len(parts)

    def store(group, product, lane):
        for k in range(blocks):
            out[k, group] = product[
                k * width : (k + 1) * width, lane * TOK_DEV : (lane + 1) * TOK_DEV
            ].astype(BF16)

    queries[...] = jnp.zeros_like(queries)
    for v in range(INNER):

        @pl.when(xy == v)
        def _(v=v):
            step = depth // INNER
            for r, piece in enumerate(pieces):
                place = (r ^ v) * step
                basis[:, place : place + step] = piece[0].astype(F32).T.astype(BF16)
            for g in range(n):
                place = ((g % INNER) ^ v) * (n // INNER) + ((g // INNER) ^ z)
                extra = parts[0][place, share:, cols].astype(F32)
                queries[g * query_rows : (g + 1) * query_rows] = extra[:query_rows]
                info[g] = extra[:, : info.shape[2]]

    store(
        n,
        lax.dot_general(
            basis[...], queries[...].astype(BF16), NT, preferred_element_type=F32
        ),
        0,
    )

    @pl.loop(0, n // INNER)
    def _(plane):
        for v in range(INNER):

            @pl.when(xy == v)
            def _(v=v):
                for p in range(INNER):
                    rows[p * TOK_DEV : (p + 1) * TOK_DEV] = gather_rows(
                        parts, e, (p ^ v) * (n // INNER) + (plane ^ z), share, cols
                    )

        product = lax.dot_general(basis[...], rows[...], NT, preferred_element_type=F32)
        for p in range(INNER):
            store(plane * INNER + p, product, p)


def rotate_in(where, pieces, parts, n, blocks, query_rows, at):
    _, width, cols = pieces[0].shape
    depth = INNER * width
    return call(
        functools.partial(rotate_in_kernel, n, blocks, query_rows, at),
        [
            jax.ShapeDtypeStruct((blocks, n + 1, cols // blocks, TOK_DEV), BF16),
            jax.ShapeDtypeStruct((n, EXTRA, 256), F32),
        ],
        where,
        *pieces,
        *parts,
        scratch=[
            pltpu.VMEM((cols, depth), BF16),
            pltpu.VMEM((INNER * TOK_DEV, depth), BF16),
            pltpu.VMEM((TOK_DEV, depth), F32),
        ],
        mib=48,
        flops=2 * (n + 1) * TOK_DEV * cols * depth,
    )


def rotate_out_kernel(chunk, outer, query_rows, where, basis, *refs):
    parts, outs = grouped(refs[:-6]), refs[-6:-2]
    rows, queries = refs[-2:]
    sx, kx, sy, ky = outs
    xy, z, e = where[0] % INNER, where[0] // INNER, where[1]
    half = outer // 2
    cols, depth = basis.shape[1], basis.shape[2]
    share = TOK_DEV // len(parts)
    total = queries.shape[0]

    for v in range(INNER):

        @pl.when((pl.program_id(0) == 0) & (xy == v))
        def _(v=v):
            for p in range(outer):
                group = chunk * outer + p
                rows[p * TOK_DEV : (p + 1) * TOK_DEV] = gather_rows(
                    [part[(p % INNER) ^ v] for part in parts],
                    e,
                    (group // INNER) ^ z,
                    share,
                    slice(0, depth),
                )
            if chunk == 0:
                for g in range(outer * INNER):
                    part = parts[0][(g % INNER) ^ v]
                    extra = part[(g // INNER) ^ z, share:, :depth].astype(F32)
                    queries[g * query_rows : (g + 1) * query_rows] = extra[:query_rows]

    product = lax.dot_general(basis[0], rows[...], NT, preferred_element_type=F32)

    def put(ref, place, first):
        for p in range(half):
            lane = (first + p) * TOK_DEV
            ref[place, p * cols : (p + 1) * cols] = product[:, lane : lane + TOK_DEV].astype(
                BF16
            )

    for r, (a, i, b, j) in enumerate(
        [(kx, 0, ky, 0), (sx, 0, ky, 1), (kx, 1, sy, 0), (sx, 1, sy, 1)]
    ):

        @pl.when(pl.program_id(0) == r)
        def _(a=a, i=i, b=b, j=j):
            put(a, i, 0)
            put(b, j, half)
            if chunk == 0:
                turned = lax.dot_general(
                    queries[...].astype(BF16), basis[0], NT, preferred_element_type=F32
                )
                rest = padded(cols) - cols
                if rest:
                    turned = jnp.concatenate([turned, jnp.zeros((total, rest), F32)], axis=1)
                for k in range(padded(cols) // 128):
                    start = half * cols + k * total
                    a[i, start : start + total] = turned[:, k * 128 : (k + 1) * 128].astype(
                        BF16
                    )


def rotate_out(where, *, basis, parts, chunk, outer, query_rows):
    _, cols, depth = basis.shape
    half = outer // 2
    total = outer * INNER * query_rows
    flat = [part for group in parts for part in group]
    extra = total * padded(cols) // 128 if chunk == 0 else 0
    first = jax.ShapeDtypeStruct((2, half * cols + extra, TOK_DEV), BF16)
    second = jax.ShapeDtypeStruct((2, half * cols, TOK_DEV), BF16)
    outs = [first, first, second, second]
    return pl.pallas_call(
        functools.partial(rotate_out_kernel, chunk, outer, query_rows),
        out_shape=outs,
        grid_spec=pltpu.PrefetchScalarGridSpec(
            num_scalar_prefetch=1,
            grid=(INNER,),
            in_specs=[pl.BlockSpec((1, cols, depth), lambda r, w: (r ^ (w[0] % INNER), 0, 0))]
            + [pl.BlockSpec(part.shape, lambda r, w: (0, 0, 0)) for part in flat],
            out_specs=[pl.BlockSpec(out.shape, lambda r, w: (0, 0, 0)) for out in outs],
            scratch_shapes=[
                pltpu.VMEM((outer * TOK_DEV, depth), BF16),
                pltpu.VMEM((total, depth), F32),
            ],
        ),
        compiler_params=pltpu.CompilerParams(vmem_limit_bytes=32 << 20),
        cost_estimate=pl.CostEstimate(
            flops=2 * outer * TOK_DEV * basis.size,
            bytes_accessed=2 * (basis.size + outer * TOK_DEV * (INNER * cols + depth)),
            transcendentals=0,
        ),
    )(where, basis, *flat)


def score_kernel(chunk, outer, masks, shares, info_row, where, b_ref, inverse, query_b, info, *refs):
    a_refs, q_refs, out, a_all = refs[:shares], refs[shares:-2], refs[-2], refs[-1]
    z, e = where[0] // INNER, where[1]
    rows, width = a_all.shape[1], a_refs[0].shape[2]
    tile = 256 if rows % 256 == 0 else 128

    def gather(sources, group, slot):
        for r in range(INNER):
            for h in range(shares):
                a = sources[0][r, group]
                for m in range(1, shares):
                    a = jnp.where((e ^ m) == h, sources[m][r, group], a)
                start = (r * shares + h) * width
                a_all[slot, start : start + width] = a

    gather(q_refs, 0, len(masks))
    for p, mask in enumerate(masks):
        place = z ^ mask
        gather(a_refs, place, p)
        seq = info[chunk * outer + place][info_row : info_row + 1, :TOK_DEV]
        for member in range(SEQ_DEV):
            b = jnp.where(seq == member, b_ref[p].astype(F32), 0.0).astype(BF16)
            total = jnp.zeros((b.shape[0], TOK_DEV), F32)
            for start in range(0, rows, tile):
                grad = lax.dot_general(
                    b, a_all[p, start : start + tile], NT, preferred_element_type=F32
                )
                scaled = (grad * inverse[:, start : start + tile]).astype(BF16)
                total = total + jnp.dot(
                    scaled,
                    a_all[len(masks), start : start + tile],
                    preferred_element_type=F32,
                )
            out[p, member : member + 1] = jnp.sum(total * query_b[...], axis=0, keepdims=True)


def score(where, b, a_parts, inverse, query_b, info, chunk, outer, masks, info_row):
    cols, rows = inverse.shape
    count = len(masks)
    _, groups, width, _ = a_parts[0].shape
    return pl.pallas_call(
        functools.partial(score_kernel, chunk, outer, masks, len(a_parts), info_row),
        out_shape=jax.ShapeDtypeStruct((count, SEQ_DEV, TOK_DEV), F32),
        grid=(1,),
        in_specs=[SMEM]
        + [VMEM] * 4
        + [pl.BlockSpec((INNER, outer, width, TOK_DEV), lambda i: (0, chunk, 0, 0))]
        * len(a_parts)
        + [pl.BlockSpec((INNER, 1, width, TOK_DEV), lambda i: (0, groups - 1, 0, 0))]
        * len(a_parts),
        out_specs=VMEM,
        scratch_shapes=[pltpu.VMEM((count + 1, rows, TOK_DEV), BF16)],
        compiler_params=pltpu.CompilerParams(vmem_limit_bytes=28 << 20),
        cost_estimate=pl.CostEstimate(
            flops=16 * count * SEQ_DEV * TOK_DEV * cols * rows,
            bytes_accessed=2 * (b.size + a_parts[0].size + 2 * inverse.size),
            transcendentals=0,
        ),
    )(where, b, inverse, query_b, info, *a_parts, *a_parts)


def body(
    train_in,
    train_out,
    query_in,
    query_out,
    input_basis,
    output_basis,
    corrected,
    train_seq,
    query_order,
):
    n, size = lax.axis_size("seq"), lax.axis_size("eig")
    outer = n // INNER
    me, e = lax.axis_index("seq"), lax.axis_index("eig")
    xy, z = me % INNER, me // INNER
    where = jnp.stack([me, e]).astype(jnp.int32)
    share = TOK_DEV // size
    query_rows = query_in.shape[0]
    queries = n * query_rows
    depth_out, cols = output_basis.shape
    cols_own = cols // INNER
    rows_own = corrected.shape[0]
    rows_in = rows_own * INNER
    per_core = input_basis.shape[1] // rows_in

    def in_plane(pieces):
        return [pieces[0]] + [swap(pieces[r], "seq", r) for r in range(1, INNER)]

    def in_turn(pieces, first, last):
        done = [swap(after(pieces[r], *first), "seq", r) for r in range(1, INNER - 1)]
        x = after(pieces[-1], *last, done[0])
        return [pieces[0]] + done + [swap(x, "seq", INNER - 1)]

    info = jnp.concatenate([train_seq, query_order % QUERIES]).astype(BF16)
    info = jnp.pad(info, (0, padded(rows_in) - info.shape[0]))[None]
    sent = pack(where, train_out, train_in, query_out, query_in, info, share, outer)
    sent = [sent[0]] + [swap(sent[m], "seq", m * INNER) for m in range(1, outer)]

    basis_pieces = in_turn(
        split(
            where,
            [after(input_basis, sent[0])],
            [
                [
                    (
                        (k * INNER + a) * rows_own,
                        (k * INNER + a + 1) * rows_own,
                        k * rows_own,
                    )
                    for k in range(per_core)
                ]
                for a in range(INNER)
            ],
        ),
        sent[1:2],
        sent[2:],
    )

    inverse = invert(
        where,
        in_turn(
            split(
                where,
                [after(corrected, sent[0])],
                [[(a * cols_own, (a + 1) * cols_own, 0)] for a in range(INNER)],
            ),
            (),
            (),
        ),
    )

    wide = padded(INNER * depth_out)
    basis_out = output_basis.reshape(depth_out, INNER, cols_own).transpose(1, 2, 0)
    *out_pieces, in_piece = split(
        after(where, inverse, basis_out, *basis_pieces[1:-1]),
        sent,
        [[(a * depth_out, (a + 1) * depth_out, 0)] for a in range(INNER)],
        (wide, wide + rows_in),
    )

    out_pieces = in_plane(out_pieces)
    parts = [out_pieces] + [
        [swap(x, "eig", m) for x in out_pieces] for m in range(1, size)
    ]
    in_rel = in_plane([after(in_piece, *out_pieces[1:], basis_pieces[-1])] * INNER)
    rotate = functools.partial(
        rotate_out, basis=basis_out, parts=parts, outer=outer, query_rows=query_rows
    )

    def plane_sum(sx, kx, sy, ky):
        rx, ry = yield (sx, 1), (sy, 2)
        low, high = yield (add(kx[1], rx[1]), 2), (add(ky[1], ry[1]), 1)
        return add(kx[0], rx[0], low), add(ky[0], ry[0], high)

    def planes_sum(held, extra=None):
        for b in bits(outer):
            bit = (z >> b) & 1
            pairs = held.reshape((-1, 2) + held.shape[1:])
            x = pick(pairs, 1 - bit, 1)
            if extra is not None:
                x = jnp.concatenate([x.reshape(-1, TOK_DEV), extra])
            (got,) = yield ((x, INNER << b),)
            if extra is not None:
                at = got.shape[0] - extra.shape[0]
                extra = add(extra, got[at:])
                got = got[:at].reshape((-1,) + held.shape[1:])
            held = add(pick(pairs, bit, 1), got)
        masks = [0]
        for b in reversed(bits(outer)):
            shape = held.shape
            flat = held.reshape(-1, TOK_DEV)
            items = [flat] if b else [flat[:16], flat[16:]]
            got = yield tuple((x, INNER << b) for x in items)
            more = [m | (1 << b) for m in masks]
            held, masks = jnp.concatenate([flat] + got), masks + more
            held = held.reshape((2 * shape[0],) + shape[1:])
        return held, masks, extra

    partial_sums = [rotate(where, chunk=0)]
    partial_sums.append(rotate(after(where, partial_sums[0][2]), chunk=1))
    in_rel = jnp.concatenate([after(x, partial_sums[0][2]) for x in in_rel])
    in_parts = [in_rel] + [swap(in_rel, "eig", m) for m in range(1, size)]
    rotated, info = rotate_in(
        after(where, partial_sums[1][2]), basis_pieces, in_parts, n, per_core, query_rows, 0
    )
    rotated = rotated.reshape(per_core, n + 1, size, rows_own // size, TOK_DEV)
    swapped = [swap(pick(rotated, e ^ m, 2), "eig", m) for m in range(1, size)]
    rotated = jnp.stack([pick(rotated, e, 2)] + swapped)
    rotated = unxor(rotated, e).reshape((outer,) + rotated.shape[2:])
    across = [[INNER * i + a for i in range(outer)] for a in range(INNER)]
    inside = [[INNER * i + a for a in range(INNER)] for i in range(outer)]
    rotated = lax.psum_scatter(
        rotated, "seq", scatter_dimension=0, tiled=True, axis_index_groups=across
    )

    def between_cores(x):
        a_parts = [x] + [swap(x, "eig", m) for m in range(1, size)]
        if a_parts[0].shape[2] % 16:
            whole = unxor(jnp.stack(a_parts), e).transpose(1, 2, 0, 3, 4)
            a_parts = [whole.reshape(INNER, n + 1, rows_own, TOK_DEV)]
        return a_parts

    active = {("plane", 0): plane_sum(*partial_sums[0])}
    got, fence, found, scored = {}, [], {}, {}
    step, query_b = 0, None
    while active:
        sends = {}
        for key in list(active):
            try:
                sends[key] = active[key].send(got.get(key))
                continue
            except StopIteration as stop:
                value = stop.value
            kind, chunk = key
            del active[key]
            if kind == "plane":
                low, high = value
                at = outer // 2 * cols_own
                held = jnp.concatenate([low[:at], high]).reshape(outer, cols_own, TOK_DEV)
                active["planes", chunk] = planes_sum(held, None if chunk else low[at:])
                sends["planes", chunk] = active["planes", chunk].send(None)
            else:
                found[chunk] = value[:2]
                if chunk == 0:
                    value = value[2].reshape(-1, queries, TOK_DEV).transpose(0, 2, 1)
                    value = value.reshape(-1, queries)[:cols_own].astype(F32)
                    query_b = jnp.pad(value, ((0, 0), (0, TOK_DEV - queries)))
        if 0 < step < INNER:
            begun = plane_sum(*partial_sums[step])
            active["plane", step] = begun
            sends["plane", step] = begun.send(None)
        if step == 2:
            fence = fence + swapped
        if step == INNER:
            gathered = lax.all_gather(
                after(rotated, *fence), "seq", axis=0, tiled=True, axis_index_groups=inside
            )
        if step == INNER + 2:
            a_parts = between_cores(after(gathered, *fence))
            fence = fence + list(a_parts)
        if 0 < step < INNER:
            fence = fence + [partial_sums[step][2]]
        got = {}
        for key, items in sends.items():
            got[key] = [swap(after(x, *fence), "seq", mask) for x, mask in items]
        if 0 < step < INNER - 1:
            partial_sums.append(rotate(after(where, *fence), chunk=step + 1))
        fence = [x for items in got.values() for x in items]
        for chunk in sorted(set(found) - set(scored)):
            held, masks = found[chunk]
            here = where
            if len(fence) > 1:
                here = after(where, min(fence, key=lambda x: x.size))
            values = score(
                here, held, a_parts, inverse, query_b, info, chunk, outer, masks, query_rows
            )
            if chunk == 0:
                fence = fence + [values]
            values = values[:, :, :queries]
            scored[chunk] = unxor(
                jnp.stack([values[masks.index(m)] for m in range(outer)]), z
            )
        step += 1
    labels = info[:, query_rows, TOK_DEV : TOK_DEV + query_rows].reshape(-1)
    hot = (labels[:, None] == jnp.arange(QUERIES, dtype=F32)[None, :]).astype(F32)
    per_token = jnp.concatenate([scored[chunk] for chunk in range(INNER)])
    scores = jnp.sum(per_token[:, :, :, None] * hot[None, None], axis=2)
    scores = lax.all_to_all(scores, "seq", split_axis=0, concat_axis=0, tiled=True)
    scores = jnp.sum(scores, axis=0)
    for b in bits(size):
        scores = scores + swap(scores, "eig", 1 << b)
    factor = 1.0 / math.sqrt(DIN * EIGOUT * (TOK_DEV / SEQ_DEV) * (queries / QUERIES))
    return scores * factor


def solution(mesh):
    placed = (
        P("seq", None),
        P("seq", None),
        P("seq", None),
        P("seq", None),
        P("seq", "eig"),
        P("seq", "eig"),
        P("seq", "eig"),
        P("seq"),
        P("seq"),
    )
    return jax.shard_map(
        body, mesh=mesh, in_specs=placed, out_specs=P("seq", None), check_vma=False
    )
```
